32 devices in a mesh: blk: 16 (over z, x, core), help: 2 (over y).
Axes of the slice: x: 2, y: 2, z: 4, core: 2. Of those that a mesh axis runs over, the one named last changes fastest.
Arguments:
- features_t: bfloat16 [256, 24576], P(None, 'blk'), may hold values from -6 to 6
- weight: bfloat16 [256, 256], replicated, may hold values from -0.375 to 0.375
- bias: float32 [256], P('help'), may hold values from -3 to 3
- cotangent_t: bfloat16 [256, 24576], P('help', 'blk'), may hold values from -6 to 6
- tile_vals: bfloat16 [16, 2, 80, 128, 128], P('blk', 'help'), may hold values from -0.15625 to 0.15625
- slot_row: int32 [16, 2, 80], P('blk', 'help'), may hold values from 0 to 12, as said below
- slot_col: int32 [16, 2, 80], P('blk', 'help'), may hold values from 0 to 59, as said below
Outputs:
- output_t: bfloat16 [256, 24576], P('help', 'blk')
- propagated_grad: float32 [256, 24576], P('help', 'blk')
- weight_grad: float32 [256, 256], P(None, 'help')
- bias_grad: float32 [256], P('help')
The draws below stay inside these ranges and needn't reach their ends.
Inputs may be any that keep to these rules, and one draw needn't show every extreme that they name: `slot_row`: each device has 80 slots, the used ones first; a slot holding 12 is unused. In every node-row block one helper uses all 80 slots and every other one at least 40. A slot's column tile is tile slot_col % 12 of node-row block (own block + slot_col // 12 - 2) taken around the loop of 16 blocks.
All inputs are finite; a program needn't handle non-finite values.
Results may differ from the reference program's by a relative error of at most 0.0045.
Values may be sent and summed in bfloat16 or wider, within the bound.
A program may use at most 64 MiB of HBM per device.

```python
import math
import jax
import jax.numpy as jnp
from jax import lax

F = 256
TILE = 128
BAND = 2
TR = 12
KD = 80
GROUPS = 16
HELPERS = 2
NODES = 24576
N_BLK = 16


def slot_plan(key):
    base = jax.random.fold_in(key, 11)
    key_perm, key_pick, key_count, key_full, key_col = jax.random.split(base, 5)
    perms = jax.vmap(lambda sub: jax.random.permutation(sub, TR))(jax.random.split(key_perm, GROUPS))
    picks = jax.random.randint(key_pick, (2, GROUPS, HELPERS, KD), 0, TR)
    ranks = jnp.minimum(picks[0], picks[1])
    spread_perms = jnp.broadcast_to(perms[:, None, :], (GROUPS, HELPERS, TR))
    rows = jnp.take_along_axis(spread_perms, ranks, axis=2)
    counts = jax.random.randint(key_count, (GROUPS, HELPERS), KD // 2, KD + 1)
    fullest = jax.random.randint(key_full, (GROUPS, 1), 0, HELPERS)
    counts = jnp.where(jnp.arange(HELPERS, dtype=jnp.int32)[None, :] == fullest, KD, counts)
    used = jnp.arange(KD, dtype=jnp.int32)[None, None, :] < counts[:, :, None]
    rows = jnp.where(used, rows, TR).astype(jnp.int32)
    cols = jax.random.randint(key_col, (GROUPS, HELPERS, KD), 0, (2 * BAND + 1) * TR).astype(jnp.int32)
    return (rows, cols)


def draw_slot_row(key, part):
    return slot_plan(key)[0]


def draw_slot_col(key, part):
    return slot_plan(key)[1]


def levels(own_key, extent, cuts, low, high):
    def one(position, blocks):
        steps = jax.random.uniform(jax.random.fold_in(jax.random.fold_in(own_key, 6), position), (blocks,), jnp.float32, low / len(cuts), high / len(cuts))
        return jnp.repeat(jnp.exp(steps), extent[position] // blocks).reshape((-1,) + (1,) * (len(extent) - position - 1))

    gain = one(*cuts[0])
    for cut in cuts[1:]:
        gain = gain * one(*cut)
    return gain


def centred(key, dims, scale, bound, cuts=(), kind=jnp.bfloat16):
    entries = jax.random.normal(key, dims, jnp.float32) * scale
    if len(cuts) > 0:
        entries = levels(key, dims, cuts, -0.22, 0.18) * entries
    return jnp.clip(entries, min=-bound, max=bound).astype(kind)


def setup_inputs(seed: int = 0) -> dict:
    key_of = jax.random.split(jax.random.key(seed), 8)
    features_t = centred(key_of[0], (F, NODES), 1.0, 6.0, ((1, 16),))
    weight = centred(key_of[1], (F, F), F ** -0.5, 0.375)
    bias = centred(key_of[2], (F,), 0.5, 3.0, ((0, 2),), jnp.float32)
    cotangent_t = centred(key_of[3], (F, NODES), 1.0, 6.0, ((0, 2), (1, 16)))
    tile_vals = centred(key_of[4], (GROUPS, HELPERS, KD, TILE, TILE), (TILE * KD * HELPERS // TR) ** -0.5, 0.15625, ((0, 16), (1, 2)))
    slot_row = draw_slot_row(jax.random.fold_in(key_of[7], 71), 0)
    slot_col = draw_slot_col(jax.random.fold_in(key_of[7], 71), 0)
    return dict(features_t=features_t, weight=weight, bias=bias, cotangent_t=cotangent_t, tile_vals=tile_vals, slot_row=slot_row, slot_col=slot_col)


def propagate(source_t, tile_vals, slot_row, slot_col):
    width = source_t.shape[0]
    tile = tile_vals.shape[-1]
    rows_block = TR * tile
    blocks = source_t.reshape(width, N_BLK, rows_block)
    offsets = jnp.arange(-BAND, BAND + 1, dtype=jnp.int32)

    def one_group(items):
        index, group_tiles, group_rows, group_cols = items
        chosen = ((index + offsets) % N_BLK).astype(jnp.int32)
        window = jnp.take(blocks, chosen, axis=1).reshape(width, (2 * BAND + 1) * rows_block)
        tiles = group_tiles.reshape(-1, tile, tile)
        rows = group_rows.reshape(-1)
        cols = group_cols.reshape(-1)
        pieces = jax.vmap(lambda column: lax.dynamic_slice_in_dim(window, column * tile, tile, 1))(cols)
        products = jnp.einsum('kfc,krc->kfr', pieces.astype(jnp.float32), tiles.astype(jnp.float32), precision=lax.Precision.HIGHEST)
        onehot = (rows[None, :] == jnp.arange(TR, dtype=jnp.int32)[:, None]).astype(jnp.float32)
        summed = jnp.einsum('tk,kfr->ftr', onehot, products, precision=lax.Precision.HIGHEST)
        return summed.reshape(width, rows_block)
    indices = jnp.arange(N_BLK, dtype=jnp.int32)
    per_group = lax.map(one_group, (indices, tile_vals, slot_row, slot_col))
    return jnp.transpose(per_group, (1, 0, 2)).reshape(width, N_BLK * rows_block)

def reference(features_t, weight, bias, cotangent_t, tile_vals, slot_row, slot_col):
    agg_t = propagate(features_t, tile_vals, slot_row, slot_col).astype(jnp.bfloat16)
    pre = jnp.dot(weight.T, agg_t, preferred_element_type=jnp.float32) + bias.astype(jnp.float32)[:, None]
    output_t = jax.nn.elu(pre).astype(jnp.bfloat16)
    slope = jnp.where(pre > 0.0, jnp.ones_like(pre), jnp.exp(jnp.minimum(pre, 0.0)))
    grad_pre = (cotangent_t.astype(jnp.float32) * slope).astype(jnp.bfloat16)
    scale = 1.0 / math.sqrt(NODES)
    weight_grad = jnp.dot(agg_t, grad_pre.T, preferred_element_type=jnp.float32) * scale
    bias_grad = lax.optimization_barrier(jnp.sum(grad_pre.astype(jnp.float32), axis=1)) * scale
    back = jnp.dot(weight, grad_pre, preferred_element_type=jnp.float32).astype(jnp.bfloat16)
    propagated_grad = propagate(back, tile_vals, slot_row, slot_col)
    return (output_t, propagated_grad, weight_grad, bias_grad)
```

```python
import functools
import math

import jax
import jax.numpy as jnp
from jax import lax
from jax.experimental import pallas as pl
from jax.experimental.pallas import tpu as pltpu
from jax.sharding import PartitionSpec as P

BAND = 2
SPANS = 2 * BAND + 1
UNROLL = 8
MESH = pl.DeviceIdType.MESH
F32 = jnp.float32
BF16 = jnp.bfloat16


def layer_kernel(
    n_blk, n_help, chunks,
    meta, feat, weight, bias, cot, tiles_hbm,
    out_ref, prop_ref, grads_ref,
    win1, win2, tiles, seg, part, part_in, part2, part2_in, bias_all, cot_all, gp_all, out_all, w_t, wg, wg_in,
    tile_sem, band_send, band_recv, core_send, core_recv, help_send, help_recv, back_send, back_recv, wg_send, wg_recv,
):
    blk = lax.axis_index("blk")
    helper = lax.axis_index("help")
    row_tiles = feat.shape[1] // tiles.shape[-1]
    tile = tiles.shape[-1]
    share = cot.shape[0]
    per = row_tiles // chunks
    steps = n_blk.bit_length() - 1
    core = lax.rem(blk, 2)
    chip = blk // 2
    odd = lax.rem(chip, 2)
    pair = blk + 2 - 4 * odd
    up = lax.rem(blk + 4, n_blk)
    down = lax.rem(blk + n_blk - 4, n_blk)
    relay_to = up + odd * (down - up)
    other = blk + 1 - 2 * core
    own_slot = BAND
    pair_slot = 4 - 4 * odd
    relay_slot = 4 * odd
    ahead_slot = 4 - 4 * core
    own_dst = 1 + 2 * core
    ahead_dst = 3 - 2 * core

    def flip(step):
        bit = 1 << step
        return blk + bit - 2 * bit * lax.rem(blk // bit, 2)

    def helper_at(distance):
        return lax.rem(helper + distance, n_help)

    peers = [up, down, pair] + [flip(s) for s in range(steps) if s != 1]
    barrier = pltpu.get_barrier_semaphore()
    for peer in peers:
        pl.semaphore_signal(barrier, inc=1, device_id={"blk": peer}, device_id_type=MESH)
    for d in range(1, n_help):
        pl.semaphore_signal(barrier, inc=1, device_id={"help": helper_at(d)}, device_id_type=MESH)
    tile_copy = pltpu.make_async_copy(tiles_hbm, tiles, tile_sem)
    tile_copy.start()

    mine = pl.ds(pl.multiple_of(helper * share, share), share)

    def span(slot, j):
        return pl.ds(slot * row_tiles + j * per, per)

    def band_copy(win, stage, kind, j):
        if kind == 0:
            src, dst, to = own_slot, relay_slot, pair
        else:
            src, dst, to = pair_slot, relay_slot, relay_to
        return pltpu.make_async_remote_copy(
            src_ref=win.at[span(src, j)], dst_ref=win.at[span(dst, j)],
            send_sem=band_send.at[stage, kind, j], recv_sem=band_recv.at[stage, kind, j],
            device_id={"blk": to}, device_id_type=MESH,
        )

    def core_copy(win, stage, kind, j):
        if kind == 0:
            src, dst = own_slot, own_dst
        else:
            src, dst = ahead_slot, ahead_dst
        return pltpu.make_async_remote_copy(
            src_ref=win.at[span(src, j)], dst_ref=win.at[span(dst, j)],
            send_sem=core_send.at[stage, kind, j], recv_sem=core_recv.at[stage, kind, j],
            device_id={"blk": other}, device_id_type=MESH,
        )

    def help_copy(src, dst, k, d):
        return pltpu.make_async_remote_copy(
            src_ref=src, dst_ref=dst, send_sem=help_send.at[k, d - 1], recv_sem=help_recv.at[k, d - 1],
            device_id={"help": helper_at(d)}, device_id_type=MESH,
        )

    def cot_copy(d):
        return help_copy(cot_all.at[:, mine, :], cot_all.at[:, mine, :], chunks, d)

    def bias_copy(d):
        return help_copy(bias_all.at[mine, :], bias_all.at[mine, :], chunks + 1, d)

    def part_copy(j, d):
        return help_copy(part.at[pl.ds(j * per, per)], part_in.at[d - 1, pl.ds(j * per, per)], j, d)

    def back_copy(j, d):
        theirs = pl.ds(pl.multiple_of(helper_at(d) * share, share), share)
        return pltpu.make_async_remote_copy(
            src_ref=part2.at[pl.ds(j * per, per), theirs, :], dst_ref=part2_in.at[d - 1, pl.ds(j * per, per)],
            send_sem=back_send.at[j, d - 1], recv_sem=back_recv.at[j, d - 1],
            device_id={"help": helper_at(d)}, device_id_type=MESH,
        )

    def wg_copy(step):
        return pltpu.make_async_remote_copy(
            src_ref=wg.at[step], dst_ref=wg_in.at[step],
            send_sem=wg_send.at[step], recv_sem=wg_recv.at[step],
            device_id={"blk": flip(step)}, device_id_type=MESH,
        )

    def lanes(t):
        return slice(t * tile, (t + 1) * tile)

    pl.semaphore_wait(barrier, len(peers) + n_help - 1)

    for j in range(chunks):
        for t in range(j * per, (j + 1) * per):
            win1[own_slot * row_tiles + t] = feat[:, lanes(t)]
        band_copy(win1, 0, 0, j).start()
    for t in range(row_tiles):
        cot_all[t, mine, :] = cot[:, lanes(t)]
    bias_all[mine, :] = bias[...]
    for d in range(1, n_help):
        cot_copy(d).start()
        bias_copy(d).start()
    for j in range(chunks):
        core_copy(win1, 0, 0, j).start()
    w_t[...] = weight[...].astype(F32).T.astype(BF16)
    wg[0] = jnp.zeros_like(wg.at[0])

    def pass_on(win, stage, j):
        band_copy(win, stage, 0, j).wait_recv()
        band_copy(win, stage, 1, j).start()

    def settle(win, stage):
        for j in range(chunks):
            band_copy(win, stage, 1, j).wait_recv()
            core_copy(win, stage, 1, j).start()
        for j in range(chunks):
            core_copy(win, stage, 0, j).wait_recv()
            core_copy(win, stage, 1, j).wait_recv()

    def aggregate(win, first, last, total):
        def body(group, total):
            for u in range(UNROLL):
                t = group * UNROLL + u
                product = lax.dot_general(
                    win[meta[1, t]], tiles[meta[0, t]], (((1,), (1,)), ((), ())), preferred_element_type=F32
                )
                total = total * meta[2, t].astype(F32) + product
                seg[t] = total
            return total

        return lax.fori_loop(first, last, body, total)

    def row_sum(r):
        return seg[meta[3, r]] * meta[4, r].astype(F32)

    groups = seg.shape[0] // UNROLL
    zero = jnp.zeros(seg.shape[1:], F32)

    for j in range(chunks):
        pass_on(win1, 0, j)
    settle(win1, 0)
    tile_copy.wait()
    aggregate(win1, 0, groups, zero)

    for j in range(chunks):
        for r in range(j * per, (j + 1) * per):
            part[r] = row_sum(r).astype(BF16)
        for d in range(1, n_help):
            part_copy(j, d).start()
    for d in range(1, n_help):
        cot_copy(d).wait_recv()
        bias_copy(d).wait_recv()

    width = weight.shape[0]
    for j in range(chunks):
        for d in range(1, n_help):
            part_copy(j, d).wait_recv()

        def dense(i, carry):
            r = j * per + i
            total = row_sum(r)
            for d in range(1, n_help):
                total = total + part_in[d - 1, r].astype(F32)
            agg = total.astype(BF16)
            pre = jnp.dot(w_t[...], agg, preferred_element_type=F32) + bias_all[...]
            ex = jnp.exp(jnp.minimum(pre, 0.0))
            out_all[r] = jnp.where(pre > 0.0, pre, ex - 1.0).astype(BF16)
            grad = (cot_all[r].astype(F32) * ex).astype(BF16)
            gp_all[r] = grad
            back = jnp.dot(weight[...], grad, preferred_element_type=F32).astype(BF16)
            win2[own_slot * row_tiles + r] = back
            held = gp_all[r, mine, :]
            wg[0, :, pl.ds(0, width)] += lax.dot_general(
                held, agg, (((1,), (1,)), ((), ())), preferred_element_type=F32
            )
            wg[0, :, pl.ds(width, tile)] += held.astype(F32)
            return carry

        lax.fori_loop(0, per, dense, 0)
        band_copy(win2, 1, 0, j).start()
        core_copy(win2, 1, 0, j).start()
        if j > 0:
            pass_on(win2, 1, j - 1)
    wg_copy(0).start()
    for t in range(row_tiles):
        out_ref[:, lanes(t)] = out_all[t, mine, :]
    pass_on(win2, 1, chunks - 1)

    def wg_turn(step):
        wg_copy(step).wait_recv()
        wg[step + 1] = wg[step] + wg_in[step]
        if step + 1 < steps:
            wg_copy(step + 1).start()

    settle(win2, 1)
    wg_turn(0)
    half = groups // 2
    total = aggregate(win2, 0, half, zero)
    wg_turn(1)
    aggregate(win2, half, groups, total)

    for j in range(chunks):
        for r in range(j * per, (j + 1) * per):
            part2[r] = row_sum(r).astype(BF16)
            prop_ref[:, lanes(r)] = seg[meta[3, r], mine, :] * meta[4, r].astype(F32)
        for d in range(1, n_help):
            back_copy(j, d).start()
    wg_turn(2)
    for j in range(chunks):
        for d in range(1, n_help):
            back_copy(j, d).wait_recv()
        for r in range(j * per, (j + 1) * per):
            for d in range(1, n_help):
                prop_ref[:, lanes(r)] += part2_in[d - 1, r].astype(F32)
    for s in range(3, steps):
        wg_turn(s)
    grads_ref[...] = wg[steps]

    for stage, win in ((0, win1), (1, win2)):
        for j in range(chunks):
            for kind in range(2):
                band_copy(win, stage, kind, j).wait_send()
                core_copy(win, stage, kind, j).wait_send()
    for d in range(1, n_help):
        cot_copy(d).wait_send()
        bias_copy(d).wait_send()
        for j in range(chunks):
            part_copy(j, d).wait_send()
            back_copy(j, d).wait_send()
    for s in range(steps):
        wg_copy(s).wait_send()


def slot_table(rows, cols, row_tiles):
    slots = rows.shape[0]
    index = jnp.arange(slots, dtype=jnp.int32)
    key = rows * slots + index
    rank = jnp.sum((key[None, :] < key[:, None]).astype(jnp.int32), axis=1)
    placed = (rank[None, :] == index[:, None]).astype(jnp.int32)
    order = jnp.sum(placed * index[None, :], axis=1)
    col = jnp.sum(placed * cols[None, :], axis=1)
    head = jnp.sum(((rows[None, :] == rows[:, None]) & (index[None, :] < index[:, None])).astype(jnp.int32), axis=1)
    keep = jnp.sum(placed * (head > 0).astype(jnp.int32)[None, :], axis=1)
    tiles = jnp.arange(slots, dtype=jnp.int32)[:, None]
    last = jnp.maximum(jnp.sum((rows[None, :] <= tiles).astype(jnp.int32), axis=1) - 1, 0)
    has = jnp.max((rows[None, :] == tiles).astype(jnp.int32), axis=1)
    table = jnp.stack([order, col, keep, last, has])
    return jnp.pad(table, ((0, 3), (0, 128 - slots)))


def per_device(n_blk, n_help, features_t, weight, bias, cotangent_t, tile_vals, slot_row, slot_col):
    tiles = tile_vals[0, 0]
    slots, tile = tiles.shape[0], tiles.shape[-1]
    width, nodes = features_t.shape
    row_tiles = nodes // tile
    share = cotangent_t.shape[0]
    chunks = 4 if row_tiles % 4 == 0 else 1
    steps = n_blk.bit_length() - 1
    peers = n_help - 1
    table = slot_table(slot_row[0, 0], slot_col[0, 0], row_tiles)
    bias_wide = jnp.broadcast_to(bias[:, None], (share, tile))
    vmem = pl.BlockSpec(memory_space=pltpu.VMEM)
    dma = pltpu.SemaphoreType.DMA
    output_t, propagated, grads = pl.pallas_call(
        functools.partial(layer_kernel, n_blk, n_help, chunks),
        out_shape=(
            jax.ShapeDtypeStruct((share, nodes), BF16),
            jax.ShapeDtypeStruct((share, nodes), F32),
            jax.ShapeDtypeStruct((share, width + tile), F32),
        ),
        in_specs=[pl.BlockSpec(memory_space=pltpu.SMEM), vmem, vmem, vmem, vmem, pl.BlockSpec(memory_space=pl.ANY)],
        out_specs=(vmem, vmem, vmem),
        scratch_shapes=[
            pltpu.VMEM((SPANS * row_tiles, width, tile), BF16),
            pltpu.VMEM((SPANS * row_tiles, width, tile), BF16),
            pltpu.VMEM((slots, tile, tile), BF16),
            pltpu.VMEM((slots, width, tile), F32),
            pltpu.VMEM((row_tiles, width, tile), BF16),
            pltpu.VMEM((peers, row_tiles, width, tile), BF16),
            pltpu.VMEM((row_tiles, width, tile), BF16),
            pltpu.VMEM((peers, row_tiles, share, tile), BF16),
            pltpu.VMEM((width, tile), F32),
            pltpu.VMEM((row_tiles, width, tile), BF16),
            pltpu.VMEM((row_tiles, width, tile), BF16),
            pltpu.VMEM((row_tiles, width, tile), BF16),
            pltpu.VMEM((width, width), BF16),
            pltpu.VMEM((steps + 1, share, width + tile), F32),
            pltpu.VMEM((steps, share, width + tile), F32),
            dma,
            dma((2, 2, chunks)),
            dma((2, 2, chunks)),
            dma((2, 2, chunks)),
            dma((2, 2, chunks)),
            dma((chunks + 2, peers)),
            dma((chunks + 2, peers)),
            dma((chunks, peers)),
            dma((chunks, peers)),
            dma((steps,)),
            dma((steps,)),
        ],
        compiler_params=pltpu.CompilerParams(
            collective_id=0, has_side_effects=True, vmem_limit_bytes=48 * 1024 * 1024
        ),
    )(table, features_t, weight, bias_wide, cotangent_t, tiles)
    scale = 1.0 / math.sqrt(nodes * n_blk)
    weight_grad = grads[:, :width].T * scale
    bias_grad = jnp.sum(grads[:, width:], axis=1) * scale
    return (output_t, propagated, weight_grad, bias_grad)


def solution(mesh):
    placed = (
        P(None, "blk"),
        P(),
        P("help"),
        P("help", "blk"),
        P("blk", "help", None, None, None),
        P("blk", "help", None),
        P("blk", "help", None),
    )
    return jax.shard_map(
        functools.partial(per_device, mesh.shape["blk"], mesh.shape["help"]),
        mesh=mesh,
        in_specs=placed,
        out_specs=(P("help", "blk"), P("help", "blk"), P(None, "help"), P("help")),
        check_vma=False,
    )
```

```python
import functools
import math

import jax
import jax.numpy as jnp
from jax import lax
from jax.experimental import pallas as pl
from jax.experimental.pallas import tpu as pltpu
from jax.sharding import PartitionSpec as P

BAND = 2
SPANS = 2 * BAND + 1
UNROLL = 8
MESH = pl.DeviceIdType.MESH
F32 = jnp.float32
BF16 = jnp.bfloat16


def layer_kernel(
    n_blk, n_help, chunks,
    meta, feat_hbm, weight_hbm, bias_hbm, cot_hbm, tiles_hbm,
    out_ref, prop_ref, grads_ref,
    feat, weight, bias_wide, cot,
    win1, win2, tiles, seg, part, part_in, part2, part2_in, bias_all, cot_all, gp_all, out_all, w_t, wg, wg_in,
    sums, feat_sem, tile_sem, weight_sem, cot_sem, bias_sem, band_send, band_recv, core_send, core_recv, help_send, help_recv, back_send, back_recv, wg_send, wg_recv,
):
    blk = lax.axis_index("blk")
    helper = lax.axis_index("help")
    row_tiles = feat.shape[1] // tiles.shape[-1]
    tile = tiles.shape[-1]
    share = out_ref.shape[0]
    per = row_tiles // chunks
    steps = n_blk.bit_length() - 1
    core = lax.rem(blk, 2)
    chip = blk // 2
    odd = lax.rem(chip, 2)
    pair = blk + 2 - 4 * odd
    up = lax.rem(blk + 4, n_blk)
    down = lax.rem(blk + n_blk - 4, n_blk)
    relay_to = up + odd * (down - up)
    other = blk + 1 - 2 * core
    own_slot = BAND
    pair_slot = 4 - 4 * odd
    relay_slot = 4 * odd
    ahead_slot = 4 - 4 * core
    own_dst = 1 + 2 * core
    ahead_dst = 3 - 2 * core

    def flip(step):
        bit = 1 << step
        return blk + bit - 2 * bit * lax.rem(blk // bit, 2)

    def helper_at(distance):
        return lax.rem(helper + distance, n_help)

    mine = pl.ds(pl.multiple_of(helper * share, share), share)

    def feat_copy(j):
        part_of = (slice(None), slice(j * per * tile, (j + 1) * per * tile))
        return pltpu.make_async_copy(feat_hbm.at[part_of], feat.at[part_of], feat_sem.at[j])

    def cot_load(t):
        return pltpu.make_async_copy(cot_hbm.at[:, lanes(t)], cot_all.at[t, mine, :], cot_sem.at[t])

    def lanes(t):
        return slice(t * tile, (t + 1) * tile)

    for j in range(chunks):
        feat_copy(j).start()
    peers = [up, down, pair] + [flip(s) for s in range(steps) if s != 1]
    barrier = pltpu.get_barrier_semaphore()
    for peer in peers:
        pl.semaphore_signal(barrier, inc=1, device_id={"blk": peer}, device_id_type=MESH)
    for d in range(1, n_help):
        pl.semaphore_signal(barrier, inc=1, device_id={"help": helper_at(d)}, device_id_type=MESH)
    tile_copy = pltpu.make_async_copy(tiles_hbm, tiles, tile_sem)
    weight_copy = pltpu.make_async_copy(weight_hbm, weight, weight_sem)
    bias_load = pltpu.make_async_copy(bias_hbm, bias_all.at[mine, :], bias_sem)

    def span(slot, j):
        return pl.ds(slot * row_tiles + j * per, per)

    def band_copy(win, stage, kind, j):
        if kind == 0:
            src, dst, to = own_slot, relay_slot, pair
        else:
            src, dst, to = pair_slot, relay_slot, relay_to
        return pltpu.make_async_remote_copy(
            src_ref=win.at[span(src, j)], dst_ref=win.at[span(dst, j)],
            send_sem=band_send.at[stage, kind, j], recv_sem=band_recv.at[stage, kind, j],
            device_id={"blk": to}, device_id_type=MESH,
        )

    def core_copy(win, stage, kind, j):
        if kind == 0:
            src, dst = own_slot, own_dst
        else:
            src, dst = ahead_slot, ahead_dst
        return pltpu.make_async_remote_copy(
            src_ref=win.at[span(src, j)], dst_ref=win.at[span(dst, j)],
            send_sem=core_send.at[stage, kind, j], recv_sem=core_recv.at[stage, kind, j],
            device_id={"blk": other}, device_id_type=MESH,
        )

    def help_copy(src, dst, k, d):
        return pltpu.make_async_remote_copy(
            src_ref=src, dst_ref=dst, send_sem=help_send.at[k, d - 1], recv_sem=help_recv.at[k, d - 1],
            device_id={"help": helper_at(d)}, device_id_type=MESH,
        )

    def cot_copy(d):
        return help_copy(cot_all.at[:, mine, :], cot_all.at[:, mine, :], chunks, d)

    def bias_copy(d):
        return help_copy(bias_all.at[mine, :], bias_all.at[mine, :], chunks + 1, d)

    def part_copy(j, d):
        return help_copy(part.at[pl.ds(j * per, per)], part_in.at[d - 1, pl.ds(j * per, per)], j, d)

    def back_copy(j, d):
        theirs = pl.ds(pl.multiple_of(helper_at(d) * share, share), share)
        return pltpu.make_async_remote_copy(
            src_ref=part2.at[pl.ds(j * per, per), theirs, :], dst_ref=part2_in.at[d - 1, pl.ds(j * per, per)],
            send_sem=back_send.at[j, d - 1], recv_sem=back_recv.at[j, d - 1],
            device_id={"help": helper_at(d)}, device_id_type=MESH,
        )

    def wg_copy(step):
        return pltpu.make_async_remote_copy(
            src_ref=wg.at[step], dst_ref=wg_in.at[step],
            send_sem=wg_send.at[step], recv_sem=wg_recv.at[step],
            device_id={"blk": flip(step)}, device_id_type=MESH,
        )

    weight_copy.start()
    bias_load.start()
    for t in range(row_tiles):
        cot_load(t).start()
    tile_copy.start()
    for j in range(chunks):
        feat_copy(j).wait()
        for t in range(j * per, (j + 1) * per):
            win1[own_slot * row_tiles + t] = feat[:, lanes(t)].T
        if j == 0:
            pl.semaphore_wait(barrier, len(peers) + n_help - 1)
        band_copy(win1, 0, 0, j).start()
    for t in range(row_tiles):
        cot_load(t).wait()
    bias_load.wait()
    for d in range(1, n_help):
        cot_copy(d).start()
        bias_copy(d).start()
    for j in range(chunks):
        core_copy(win1, 0, 0, j).start()
    weight_copy.wait()
    w_t[...] = weight[...].T
    wg[0] = jnp.zeros_like(wg.at[0])

    def pass_on(win, stage, j):
        band_copy(win, stage, 0, j).wait_recv()
        band_copy(win, stage, 1, j).start()

    def settle(win, stage):
        for j in range(chunks):
            band_copy(win, stage, 1, j).wait_recv()
            core_copy(win, stage, 1, j).start()
        for j in range(chunks):
            core_copy(win, stage, 0, j).wait_recv()
            core_copy(win, stage, 1, j).wait_recv()

    def aggregate(win, first, last, total):
        def body(group, total):
            for u in range(UNROLL):
                t = group * UNROLL + u
                product = jnp.dot(tiles[meta[0, t]], win[meta[1, t]], preferred_element_type=F32)
                total = total * meta[2, t].astype(F32) + product
                seg[t] = total
            return total

        return lax.fori_loop(first, last, body, total)

    def row_sum(r):
        return seg[meta[3, r]] * meta[4, r].astype(F32)

    groups = seg.shape[0] // UNROLL
    zero = jnp.zeros(seg.shape[1:], F32)

    for j in range(chunks):
        pass_on(win1, 0, j)
    settle(win1, 0)
    tile_copy.wait()
    aggregate(win1, 0, groups, zero)

    for j in range(chunks):
        for r in range(j * per, (j + 1) * per):
            part[r] = row_sum(r).astype(BF16)
        for d in range(1, n_help):
            part_copy(j, d).start()
    for d in range(1, n_help):
        cot_copy(d).wait_recv()
        bias_copy(d).wait_recv()

    width = weight.shape[0]
    for t in range(row_tiles):
        cot[t] = cot_all[t].T
    bias_wide[...] = bias_all[...].T
    for j in range(chunks):
        for d in range(1, n_help):
            part_copy(j, d).wait_recv()
        for r in range(j * per, (j + 1) * per):
            total = row_sum(r)
            for d in range(1, n_help):
                total = total + part_in[d - 1, r].astype(F32)
            agg = total.astype(BF16)
            pre = jnp.dot(agg, weight[...], preferred_element_type=F32) + bias_wide[...]
            ex = jnp.exp(jnp.minimum(pre, 0.0))
            grad = (cot[r].astype(F32) * ex).astype(BF16)
            win2[own_slot * row_tiles + r] = jnp.dot(grad, w_t[...], preferred_element_type=F32).astype(BF16)
            out_all[r] = jnp.where(pre > 0.0, pre, ex - 1.0).astype(BF16).T
            gp_all[r] = grad.T
            held = gp_all[r, mine, :]
            wg[0, :, pl.ds(0, width)] += jnp.dot(held, agg, preferred_element_type=F32)
            wg[0, :, pl.ds(width, tile)] += held.astype(F32)
        band_copy(win2, 1, 0, j).start()
        core_copy(win2, 1, 0, j).start()
        if j > 0:
            pass_on(win2, 1, j - 1)
    wg_copy(0).start()
    for t in range(row_tiles):
        out_ref[:, lanes(t)] = out_all[t, mine, :]
    pass_on(win2, 1, chunks - 1)

    def wg_turn(step):
        wg_copy(step).wait_recv()
        wg[step + 1] = wg[step] + wg_in[step]
        if step + 1 < steps:
            wg_copy(step + 1).start()

    settle(win2, 1)
    wg_turn(0)
    half = groups // 2
    total = aggregate(win2, 0, half, zero)
    wg_turn(1)
    aggregate(win2, half, groups, total)

    for j in range(chunks):
        for r in range(j * per, (j + 1) * per):
            turned = row_sum(r).T
            part2[r] = turned.astype(BF16)
            sums[r] = turned
            prop_ref[:, lanes(r)] = sums[r, mine, :]
        for d in range(1, n_help):
            back_copy(j, d).start()
    wg_turn(2)
    for j in range(chunks):
        for d in range(1, n_help):
            back_copy(j, d).wait_recv()
        for r in range(j * per, (j + 1) * per):
            for d in range(1, n_help):
                prop_ref[:, lanes(r)] += part2_in[d - 1, r].astype(F32)
    for s in range(3, steps):
        wg_turn(s)
    grads_ref[...] = wg[steps]

    for stage, win in ((0, win1), (1, win2)):
        for j in range(chunks):
            for kind in range(2):
                band_copy(win, stage, kind, j).wait_send()
                core_copy(win, stage, kind, j).wait_send()
    for d in range(1, n_help):
        cot_copy(d).wait_send()
        bias_copy(d).wait_send()
        for j in range(chunks):
            part_copy(j, d).wait_send()
            back_copy(j, d).wait_send()
    for s in range(steps):
        wg_copy(s).wait_send()


def slot_table(rows, cols, row_tiles):
    slots = rows.shape[0]
    index = jnp.arange(slots, dtype=jnp.int32)
    key = rows * slots + index
    rank = jnp.sum((key[None, :] < key[:, None]).astype(jnp.int32), axis=1)
    placed = (rank[None, :] == index[:, None]).astype(jnp.int32)
    order = jnp.sum(placed * index[None, :], axis=1)
    col = jnp.sum(placed * cols[None, :], axis=1)
    head = jnp.sum(((rows[None, :] == rows[:, None]) & (index[None, :] < index[:, None])).astype(jnp.int32), axis=1)
    keep = jnp.sum(placed * (head > 0).astype(jnp.int32)[None, :], axis=1)
    tiles = jnp.arange(slots, dtype=jnp.int32)[:, None]
    last = jnp.maximum(jnp.sum((rows[None, :] <= tiles).astype(jnp.int32), axis=1) - 1, 0)
    has = jnp.max((rows[None, :] == tiles).astype(jnp.int32), axis=1)
    table = jnp.stack([order, col, keep, last, has])
    return jnp.pad(table, ((0, 3), (0, 128 - slots)))


def per_device(n_blk, n_help, features_t, weight, bias, cotangent_t, tile_vals, slot_row, slot_col):
    tiles = tile_vals[0, 0]
    slots, tile = tiles.shape[0], tiles.shape[-1]
    width, nodes = features_t.shape
    row_tiles = nodes // tile
    share = cotangent_t.shape[0]
    chunks = row_tiles // 2 if row_tiles % 2 == 0 else row_tiles
    steps = n_blk.bit_length() - 1
    peers = n_help - 1
    table = slot_table(slot_row[0, 0], slot_col[0, 0], row_tiles)
    bias_wide = jnp.broadcast_to(bias[:, None], (share, tile))
    vmem = pl.BlockSpec(memory_space=pltpu.VMEM)
    dma = pltpu.SemaphoreType.DMA
    output_t, propagated, grads = pl.pallas_call(
        functools.partial(layer_kernel, n_blk, n_help, chunks),
        out_shape=(
            jax.ShapeDtypeStruct((share, nodes), BF16),
            jax.ShapeDtypeStruct((share, nodes), F32),
            jax.ShapeDtypeStruct((share, width + tile), F32),
        ),
        in_specs=[pl.BlockSpec(memory_space=pltpu.SMEM)] + [pl.BlockSpec(memory_space=pl.ANY)] * 5,
        out_specs=(vmem, vmem, vmem),
        scratch_shapes=[
            pltpu.VMEM((width, nodes), BF16),
            pltpu.VMEM((width, width), BF16),
            pltpu.VMEM((tile, width), F32),
            pltpu.VMEM((row_tiles, tile, width), BF16),
            pltpu.VMEM((SPANS * row_tiles, tile, width), BF16),
            pltpu.VMEM((SPANS * row_tiles, tile, width), BF16),
            pltpu.VMEM((slots, tile, tile), BF16),
            pltpu.VMEM((slots, tile, width), F32),
            pltpu.VMEM((row_tiles, tile, width), BF16),
            pltpu.VMEM((peers, row_tiles, tile, width), BF16),
            pltpu.VMEM((row_tiles, width, tile), BF16),
            pltpu.VMEM((peers, row_tiles, share, tile), BF16),
            pltpu.VMEM((width, tile), F32),
            pltpu.VMEM((row_tiles, width, tile), BF16),
            pltpu.VMEM((row_tiles, width, tile), BF16),
            pltpu.VMEM((row_tiles, width, tile), BF16),
            pltpu.VMEM((width, width), BF16),
            pltpu.VMEM((steps + 1, share, width + tile), F32),
            pltpu.VMEM((steps, share, width + tile), F32),
            pltpu.VMEM((row_tiles, width, tile), F32),
            dma((chunks,)),
            dma,
            dma,
            dma((row_tiles,)),
            dma,
            dma((2, 2, chunks)),
            dma((2, 2, chunks)),
            dma((2, 2, chunks)),
            dma((2, 2, chunks)),
            dma((chunks + 2, peers)),
            dma((chunks + 2, peers)),
            dma((chunks, peers)),
            dma((chunks, peers)),
            dma((steps,)),
            dma((steps,)),
        ],
        compiler_params=pltpu.CompilerParams(
            collective_id=0, has_side_effects=True, vmem_limit_bytes=60 * 1024 * 1024
        ),
    )(table, features_t, weight, bias_wide, cotangent_t, tiles)
    scale = 1.0 / math.sqrt(nodes * n_blk)
    weight_grad = grads[:, :width].T * scale
    bias_grad = jnp.sum(grads[:, width:], axis=1) * scale
    return (output_t, propagated, weight_grad, bias_grad)


def solution(mesh):
    placed = (
        P(None, "blk"),
        P(),
        P("help"),
        P("help", "blk"),
        P("blk", "help", None, None, None),
        P("blk", "help", None),
        P("blk", "help", None),
    )
    return jax.shard_map(
        functools.partial(per_device, mesh.shape["blk"], mesh.shape["help"]),
        mesh=mesh,
        in_specs=placed,
        out_specs=(P("help", "blk"), P("help", "blk"), P(None, "help"), P("help")),
        check_vma=False,
    )
```

```python
import functools
import math

import jax
import jax.numpy as jnp
from jax import lax
from jax.experimental import pallas as pl
from jax.experimental.pallas import tpu as pltpu
from jax.sharding import PartitionSpec as P

BAND = 2
SPANS = 2 * BAND + 1
UNROLL = 8
HALVES = 2
VMEM_MIB = 60
MESH = pl.DeviceIdType.MESH
F32 = jnp.float32
BF16 = jnp.bfloat16


def layer_kernel(
    n_blk, n_help, chunks,
    rows_hbm, cols_hbm, feat_hbm, weight_hbm, bias_hbm, cot_hbm, tiles_hbm,
    out_ref, prop_ref, grads_ref,
    rows, cols, bias, table, meta, feat, weight, bias_wide, cot,
    win1a, win1b, win2a, win2b, tiles, seg, part, part_in, part2, part2_in, bias_all, cot_all, gp_all, out_all, w_t, wg, wg_in,
    sums, small_sem, feat_sem, tile_sem, weight_sem, cot_sem,
    band_send, band_recv, core_send, core_recv, help_send, help_recv, side_send, side_recv,
    back_send, back_recv, wg_send, wg_recv,
):
    blk = lax.axis_index("blk")
    helper = lax.axis_index("help")
    row_tiles = feat.shape[1] // tiles.shape[-1]
    slots = tiles.shape[0]
    tile = tiles.shape[-1]
    width = weight.shape[0]
    half = width // HALVES
    share = out_ref.shape[0]
    per = row_tiles // chunks
    steps = n_blk.bit_length() - 1
    core = lax.rem(blk, 2)
    chip = blk // 2
    odd = lax.rem(chip, 2)
    pair = blk + 2 - 4 * odd
    up = lax.rem(blk + 4, n_blk)
    down = lax.rem(blk + n_blk - 4, n_blk)
    relay_to = up + odd * (down - up)
    other = blk + 1 - 2 * core
    own_slot = BAND
    pair_slot = 4 - 4 * odd
    relay_slot = 4 * odd
    ahead_slot = 4 - 4 * core
    own_dst = 1 + 2 * core
    ahead_dst = 3 - 2 * core
    own_half = (helper * share) // half
    turn_half = (1 - own_half, own_half)
    win1, win2 = (win1a, win1b), (win2a, win2b)

    def flip(step):
        bit = 1 << step
        return blk + bit - 2 * bit * lax.rem(blk // bit, 2)

    def helper_at(distance):
        return lax.rem(helper + distance, n_help)

    def lanes(t):
        return slice(t * tile, (t + 1) * tile)

    mine = pl.ds(pl.multiple_of(helper * share, share), share)

    def feat_copy(h, j):
        piece = (slice(h * half, (h + 1) * half), slice(j * per * tile, (j + 1) * per * tile))
        return pltpu.make_async_copy(feat_hbm.at[piece], feat.at[piece], feat_sem.at[h, j])

    def cot_load(t):
        return pltpu.make_async_copy(cot_hbm.at[:, lanes(t)], cot_all.at[t, mine, :], cot_sem.at[t])

    for h in range(HALVES):
        for j in range(chunks):
            feat_copy(h, j).start()
    peers = [up, down, pair] + [flip(s) for s in range(steps) if s != 1]
    barrier = pltpu.get_barrier_semaphore()
    for peer in peers:
        pl.semaphore_signal(barrier, inc=1, device_id={"blk": peer}, device_id_type=MESH)
    for d in range(1, n_help):
        pl.semaphore_signal(barrier, inc=1, device_id={"help": helper_at(d)}, device_id_type=MESH)
    small = [
        pltpu.make_async_copy(rows_hbm, rows, small_sem.at[0]),
        pltpu.make_async_copy(cols_hbm, cols, small_sem.at[1]),
        pltpu.make_async_copy(bias_hbm, bias, small_sem.at[2]),
    ]
    table_copy = pltpu.make_async_copy(table, meta, small_sem.at[3])
    tile_copy = pltpu.make_async_copy(tiles_hbm, tiles, tile_sem)
    weight_copy = pltpu.make_async_copy(weight_hbm, weight, weight_sem)

    def span(slot, j):
        return pl.ds(slot * row_tiles + j * per, per)

    def band_copy(win, stage, kind, turn, j):
        if kind == 0:
            src, dst, to = own_slot, relay_slot, pair
        else:
            src, dst, to = pair_slot, relay_slot, relay_to
        return pltpu.make_async_remote_copy(
            src_ref=win[turn].at[span(src, j)], dst_ref=win[turn].at[span(dst, j)],
            send_sem=band_send.at[stage, kind, turn, j], recv_sem=band_recv.at[stage, kind, turn, j],
            device_id={"blk": to}, device_id_type=MESH,
        )

    def core_copy(win, stage, kind, turn, j):
        if kind == 0:
            src, dst = own_slot, own_dst
        else:
            src, dst = ahead_slot, ahead_dst
        return pltpu.make_async_remote_copy(
            src_ref=win[turn].at[span(src, j)], dst_ref=win[turn].at[span(dst, j)],
            send_sem=core_send.at[stage, kind, turn, j], recv_sem=core_recv.at[stage, kind, turn, j],
            device_id={"blk": other}, device_id_type=MESH,
        )

    def side_copy(ref, k, d):
        return pltpu.make_async_remote_copy(
            src_ref=ref, dst_ref=ref, send_sem=side_send.at[k, d - 1], recv_sem=side_recv.at[k, d - 1],
            device_id={"help": helper_at(d)}, device_id_type=MESH,
        )

    def cot_copy(d):
        return side_copy(cot_all.at[:, mine, :], 0, d)

    def bias_copy(d):
        return side_copy(bias_all.at[mine, :], 1, d)

    def part_copy(h, j, d):
        piece = pl.ds(j * per, per)
        return pltpu.make_async_remote_copy(
            src_ref=part.at[h, piece], dst_ref=part_in.at[d - 1, h, piece],
            send_sem=help_send.at[h, j, d - 1], recv_sem=help_recv.at[h, j, d - 1],
            device_id={"help": helper_at(d)}, device_id_type=MESH,
        )

    def back_copy(j, d):
        theirs = pl.ds(pl.multiple_of(helper_at(d) * share, share), share)
        piece = pl.ds(j * per, per)
        return pltpu.make_async_remote_copy(
            src_ref=part2.at[piece, theirs, :], dst_ref=part2_in.at[d - 1, piece],
            send_sem=back_send.at[j, d - 1], recv_sem=back_recv.at[j, d - 1],
            device_id={"help": helper_at(d)}, device_id_type=MESH,
        )

    def wg_copy(step):
        return pltpu.make_async_remote_copy(
            src_ref=wg.at[step], dst_ref=wg_in.at[step],
            send_sem=wg_send.at[step], recv_sem=wg_recv.at[step],
            device_id={"blk": flip(step)}, device_id_type=MESH,
        )

    for copy in small:
        copy.start()
    weight_copy.start()
    for t in range(row_tiles):
        cot_load(t).start()
    tile_copy.start()
    for h in range(HALVES):
        for j in range(chunks):
            feat_copy(h, j).wait()
            for t in range(j * per, (j + 1) * per):
                win1[h][own_slot * row_tiles + t] = feat[h * half : (h + 1) * half, lanes(t)].T
            if h == 0 and j == 0:
                pl.semaphore_wait(barrier, len(peers) + n_help - 1)
            band_copy(win1, 0, 0, h, j).start()
        for j in range(chunks):
            core_copy(win1, 0, 0, h, j).start()
    for copy in small:
        copy.wait()
    fill_table(rows, cols, table)
    table_copy.start()
    across = lax.broadcasted_iota(jnp.int32, (share, share), 1)
    along = lax.broadcasted_iota(jnp.int32, (share, share), 0)
    spread = jnp.sum(jnp.where(across == along, bias[...], 0.0), axis=1, keepdims=True)
    bias_all[mine, :] = jnp.broadcast_to(spread, (share, tile))
    for t in range(row_tiles):
        cot_load(t).wait()
    for d in range(1, n_help):
        cot_copy(d).start()
        bias_copy(d).start()
    weight_copy.wait()
    for h, place in ((0, turn_half[0]), (1, own_half)):
        w_t[:, pl.ds(pl.multiple_of(place * half, half), half)] = weight[h * half : (h + 1) * half, :].T
    wg[0] = jnp.zeros_like(wg.at[0])

    def pass_on(win, stage, turn, j):
        band_copy(win, stage, 0, turn, j).wait_recv()
        band_copy(win, stage, 1, turn, j).start()

    def settle(win, stage, turn):
        for j in range(chunks):
            band_copy(win, stage, 1, turn, j).wait_recv()
            core_copy(win, stage, 1, turn, j).start()
        for j in range(chunks):
            core_copy(win, stage, 0, turn, j).wait_recv()
            core_copy(win, stage, 1, turn, j).wait_recv()

    groups = slots // UNROLL
    marks = [i * groups // chunks for i in range(chunks + 1)]

    def aggregate(win, turn, between):
        def body(group, total):
            for u in range(UNROLL):
                t = group * UNROLL + u
                product = jnp.dot(tiles[meta[0, t]], win[turn][meta[1, t]], preferred_element_type=F32)
                total = total * meta[2, t].astype(F32) + product
                seg[turn, t] = total
            return total

        total = jnp.zeros((tile, half), F32)
        for i in range(chunks):
            total = lax.fori_loop(marks[i], marks[i + 1], body, total)
            between(i)

    def row_sum(turn, r):
        return seg[turn, meta[3, r]] * meta[4, r].astype(F32)

    def nothing(i):
        pass

    def send_part(h):
        for j in range(chunks):
            for r in range(j * per, (j + 1) * per):
                part[h, r] = row_sum(h, r).astype(BF16)
            for d in range(1, n_help):
                part_copy(h, j, d).start()

    for j in range(chunks):
        pass_on(win1, 0, 0, j)
    settle(win1, 0, 0)
    tile_copy.wait()
    table_copy.wait()
    aggregate(win1, 0, lambda i: pass_on(win1, 0, 1, i))
    send_part(0)
    for d in range(1, n_help):
        cot_copy(d).wait_recv()
        bias_copy(d).wait_recv()
    for t in range(row_tiles):
        cot[t] = cot_all[t].T
    bias_wide[...] = bias_all[...].T
    settle(win1, 0, 1)
    aggregate(win1, 1, nothing)
    send_part(1)

    for j in range(chunks):
        for h in range(HALVES):
            for d in range(1, n_help):
                part_copy(h, j, d).wait_recv()
        for r in range(j * per, (j + 1) * per):
            pieces = []
            for h in range(HALVES):
                total = row_sum(h, r)
                for d in range(1, n_help):
                    total = total + part_in[d - 1, h, r].astype(F32)
                pieces.append(total.astype(BF16))
            agg = jnp.concatenate(pieces, axis=1)
            pre = jnp.dot(agg, weight[...], preferred_element_type=F32) + bias_wide[...]
            ex = jnp.exp(jnp.minimum(pre, 0.0))
            grad = (cot[r].astype(F32) * ex).astype(BF16)
            back = jnp.dot(grad, w_t[...], preferred_element_type=F32).astype(BF16)
            for h in range(HALVES):
                win2[h][own_slot * row_tiles + r] = back[:, h * half : (h + 1) * half]
            out_all[r] = jnp.where(pre > 0.0, pre, ex - 1.0).astype(BF16).T
            gp_all[r] = grad.T
            held = gp_all[r, mine, :]
            wg[0, :, pl.ds(0, width)] += jnp.dot(held, agg, preferred_element_type=F32)
            wg[0, :, pl.ds(width, tile)] += held.astype(F32)
        band_copy(win2, 1, 0, 0, j).start()
        core_copy(win2, 1, 0, 0, j).start()
        if j > 0:
            pass_on(win2, 1, 0, j - 1)
    for j in range(chunks):
        band_copy(win2, 1, 0, 1, j).start()
        core_copy(win2, 1, 0, 1, j).start()
    pass_on(win2, 1, 0, chunks - 1)
    wg_copy(0).start()
    for t in range(row_tiles):
        out_ref[:, lanes(t)] = out_all[t, mine, :]

    def wg_turn(step):
        wg_copy(step).wait_recv()
        wg[step + 1] = wg[step] + wg_in[step]
        if step + 1 < steps:
            wg_copy(step + 1).start()

    def keep_sums(turn, early):
        for j in range(chunks):
            for r in range(j * per, (j + 1) * per):
                turned = row_sum(turn, r).T
                place = pl.ds(pl.multiple_of(turn_half[turn] * half, half), half)
                part2[r, place, :] = turned.astype(BF16)
                sums[r, place, :] = turned
            if early:
                for d in range(1, n_help):
                    back_copy(j, d).start()

    settle(win2, 1, 0)
    wg_turn(0)
    aggregate(win2, 0, lambda i: pass_on(win2, 1, 1, i))
    keep_sums(0, n_help == HALVES)
    wg_turn(1)
    settle(win2, 1, 1)
    aggregate(win2, 1, nothing)
    wg_turn(2)
    keep_sums(1, n_help != HALVES)
    for j in range(chunks):
        for d in range(1, n_help):
            back_copy(j, d).wait_recv()
        for r in range(j * per, (j + 1) * per):
            total = sums[r, mine, :]
            for d in range(1, n_help):
                total = total + part2_in[d - 1, r].astype(F32)
            prop_ref[:, lanes(r)] = total
    for s in range(3, steps):
        wg_turn(s)
    grads_ref[...] = wg[steps]

    for stage, win in ((0, win1), (1, win2)):
        for j in range(chunks):
            for kind in range(2):
                for turn in range(HALVES):
                    band_copy(win, stage, kind, turn, j).wait_send()
                    core_copy(win, stage, kind, turn, j).wait_send()
    for d in range(1, n_help):
        cot_copy(d).wait_send()
        bias_copy(d).wait_send()
        for j in range(chunks):
            for h in range(HALVES):
                part_copy(h, j, d).wait_send()
            back_copy(j, d).wait_send()
    for s in range(steps):
        wg_copy(s).wait_send()


def fill_table(rows, cols, table):
    slots = rows.shape[1]
    shape = (slots, slots)
    here = lax.broadcasted_iota(jnp.int32, shape, 0)
    there = lax.broadcasted_iota(jnp.int32, shape, 1)
    zero = jnp.zeros(shape, jnp.int32)
    one = zero + 1

    def upright(line):
        return jnp.sum(jnp.where(here == there, line, zero), axis=1, keepdims=True)

    def flat(mask, values):
        return jnp.sum(jnp.where(mask, values, zero), axis=0, keepdims=True)

    row_l = jnp.broadcast_to(rows[...], shape)
    row_s = jnp.broadcast_to(upright(row_l), shape)
    col_s = jnp.broadcast_to(upright(jnp.broadcast_to(cols[...], shape)), shape)
    before = row_l * slots + there < row_s * slots + here
    rank = jnp.broadcast_to(jnp.sum(jnp.where(before, one, zero), axis=1, keepdims=True), shape)
    placed = rank == there
    table[...] = jnp.zeros(table.shape, jnp.int32)
    table[0:1, 0:slots] = flat(placed, here)
    table[1:2, 0:slots] = flat(placed, col_s)
    goes_on = flat(placed, row_s) == flat(rank + 1 == there, row_s)
    table[2:3, 0:slots] = jnp.where(goes_on, 1, 0)
    table[3:4, 0:slots] = jnp.maximum(flat(row_s <= there, one) - 1, 0)
    table[4:5, 0:slots] = jnp.minimum(flat(row_s == there, one), 1)


def per_device(n_blk, n_help, features_t, weight, bias, cotangent_t, tile_vals, slot_row, slot_col):
    tiles = tile_vals[0, 0]
    slots, tile = tiles.shape[0], tiles.shape[-1]
    width, nodes = features_t.shape
    half = width // HALVES
    row_tiles = nodes // tile
    share = cotangent_t.shape[0]
    chunks = 4 if row_tiles % 4 == 0 else 1
    steps = n_blk.bit_length() - 1
    peers = n_help - 1
    vmem = pl.BlockSpec(memory_space=pltpu.VMEM)
    dma = pltpu.SemaphoreType.DMA
    output_t, propagated, grads = pl.pallas_call(
        functools.partial(layer_kernel, n_blk, n_help, chunks),
        out_shape=(
            jax.ShapeDtypeStruct((share, nodes), BF16),
            jax.ShapeDtypeStruct((share, nodes), F32),
            jax.ShapeDtypeStruct((share, width + tile), F32),
        ),
        in_specs=[pl.BlockSpec(memory_space=pltpu.HBM)] * 7,
        out_specs=(vmem, vmem, vmem),
        scratch_shapes=[
            pltpu.VMEM((1, slots), jnp.int32),
            pltpu.VMEM((1, slots), jnp.int32),
            pltpu.VMEM((1, share), F32),
            pltpu.VMEM((8, 128), jnp.int32),
            pltpu.SMEM((8, 128), jnp.int32),
            pltpu.VMEM((width, nodes), BF16),
            pltpu.VMEM((width, width), BF16),
            pltpu.VMEM((tile, width), F32),
            pltpu.VMEM((row_tiles, tile, width), BF16),
            *[pltpu.VMEM((SPANS * row_tiles, tile, half), BF16)] * (2 * HALVES),
            pltpu.VMEM((slots, tile, tile), BF16),
            pltpu.VMEM((HALVES, slots, tile, half), F32),
            pltpu.VMEM((HALVES, row_tiles, tile, half), BF16),
            pltpu.VMEM((peers, HALVES, row_tiles, tile, half), BF16),
            pltpu.VMEM((row_tiles, width, tile), BF16),
            pltpu.VMEM((peers, row_tiles, share, tile), BF16),
            pltpu.VMEM((width, tile), F32),
            pltpu.VMEM((row_tiles, width, tile), BF16),
            pltpu.VMEM((row_tiles, width, tile), BF16),
            pltpu.VMEM((row_tiles, width, tile), BF16),
            pltpu.VMEM((width, width), BF16),
            pltpu.VMEM((steps + 1, share, width + tile), F32),
            pltpu.VMEM((steps, share, width + tile), F32),
            pltpu.VMEM((row_tiles, width, tile), F32),
            dma((4,)),
            dma((HALVES, chunks)),
            dma,
            dma,
            dma((row_tiles,)),
            dma((2, 2, HALVES, chunks)),
            dma((2, 2, HALVES, chunks)),
            dma((2, 2, HALVES, chunks)),
            dma((2, 2, HALVES, chunks)),
            dma((HALVES, chunks, peers)),
            dma((HALVES, chunks, peers)),
            dma((2, peers)),
            dma((2, peers)),
            dma((chunks, peers)),
            dma((chunks, peers)),
            dma((steps,)),
            dma((steps,)),
        ],
        compiler_params=pltpu.CompilerParams(
            collective_id=0, has_side_effects=True, vmem_limit_bytes=VMEM_MIB * 1024 * 1024
        ),
    )(slot_row[0], slot_col[0], features_t, weight, bias.reshape(1, share), cotangent_t, tiles)
    scale = 1.0 / math.sqrt(nodes * n_blk)
    weight_grad = grads[:, :width].T * scale
    bias_grad = jnp.sum(grads[:, width:], axis=1) * scale
    return (output_t, propagated, weight_grad, bias_grad)


def solution(mesh):
    placed = (
        P(None, "blk"),
        P(),
        P("help"),
        P("help", "blk"),
        P("blk", "help", None, None, None),
        P("blk", "help", None),
        P("blk", "help", None),
    )
    return jax.shard_map(
        functools.partial(per_device, mesh.shape["blk"], mesh.shape["help"]),
        mesh=mesh,
        in_specs=placed,
        out_specs=(P("help", "blk"), P("help", "blk"), P(None, "help"), P("help")),
        check_vma=False,
    )
```

```python
import functools
import math

import jax
import jax.numpy as jnp
from jax import lax
from jax.experimental import pallas as pl
from jax.experimental.pallas import tpu as pltpu
from jax.sharding import PartitionSpec as P

BAND = 2
SPANS = 2 * BAND + 1
UNROLL = 8
HALVES = 2
AHEAD = 2
VMEM_MIB = 60
MESH = pl.DeviceIdType.MESH
F32 = jnp.float32
BF16 = jnp.bfloat16


def layer_kernel(
    n_blk, n_help, chunks,
    rows_hbm, cols_hbm, feat_hbm, weight_hbm, bias_hbm, cot_hbm, tiles_hbm,
    out_ref, prop_ref, grads_ref,
    rows, cols, bias, table, meta, feat, weight, bias_wide, cot,
    win1a, win1b, win2a, win2b, tiles, seg, part, part_in, part2, part2_in, bias_all, cot_all, gp_all, out_all, w_t, wg, wg_in,
    sums, small_sem, feat_sem, tile_sem, weight_sem, cot_sem,
    band_send, band_recv, core_send, core_recv, help_send, help_recv, side_send, side_recv,
    back_send, back_recv, wg_send, wg_recv,
):
    blk = lax.axis_index("blk")
    helper = lax.axis_index("help")
    row_tiles = feat.shape[1] // tiles.shape[-1]
    slots = tiles.shape[0]
    tile = tiles.shape[-1]
    width = weight.shape[0]
    half = width // HALVES
    share = out_ref.shape[0]
    per = row_tiles // chunks
    steps = n_blk.bit_length() - 1
    core = lax.rem(blk, 2)
    chip = blk // 2
    odd = lax.rem(chip, 2)
    pair = blk + 2 - 4 * odd
    up = lax.rem(blk + 4, n_blk)
    down = lax.rem(blk + n_blk - 4, n_blk)
    relay_to = up + odd * (down - up)
    other = blk + 1 - 2 * core
    own_slot = BAND
    pair_slot = 4 - 4 * odd
    relay_slot = 4 * odd
    ahead_slot = 4 - 4 * core
    own_dst = 1 + 2 * core
    ahead_dst = 3 - 2 * core
    own_half = (helper * share) // half
    turn_half = (1 - own_half, own_half)
    win1, win2 = (win1a, win1b), (win2a, win2b)

    def flip(step):
        bit = 1 << step
        return blk + bit - 2 * bit * lax.rem(blk // bit, 2)

    def helper_at(distance):
        return lax.rem(helper + distance, n_help)

    def lanes(t):
        return slice(t * tile, (t + 1) * tile)

    mine = pl.ds(pl.multiple_of(helper * share, share), share)

    def feat_copy(h, j):
        piece = (slice(h * half, (h + 1) * half), slice(j * per * tile, (j + 1) * per * tile))
        return pltpu.make_async_copy(feat_hbm.at[piece], feat.at[piece], feat_sem.at[h, j])

    def cot_load(t):
        return pltpu.make_async_copy(cot_hbm.at[:, lanes(t)], cot_all.at[t, mine, :], cot_sem.at[t])

    for h in range(HALVES):
        for j in range(chunks):
            feat_copy(h, j).start()
    peers = [up, down, pair] + [flip(s) for s in range(steps) if s != 1]
    barrier = pltpu.get_barrier_semaphore()
    for peer in peers:
        pl.semaphore_signal(barrier, inc=1, device_id={"blk": peer}, device_id_type=MESH)
    for d in range(1, n_help):
        pl.semaphore_signal(barrier, inc=1, device_id={"help": helper_at(d)}, device_id_type=MESH)
    small = [
        pltpu.make_async_copy(rows_hbm, rows, small_sem.at[0]),
        pltpu.make_async_copy(cols_hbm, cols, small_sem.at[1]),
        pltpu.make_async_copy(bias_hbm, bias, small_sem.at[2]),
    ]
    table_copy = pltpu.make_async_copy(table, meta, small_sem.at[3])
    tile_copy = pltpu.make_async_copy(tiles_hbm, tiles, tile_sem)
    weight_copy = pltpu.make_async_copy(weight_hbm, weight, weight_sem)

    def span(slot, j):
        return pl.ds(slot * row_tiles + j * per, per)

    def band_copy(win, stage, kind, turn, j):
        if kind == 0:
            src, dst, to = own_slot, relay_slot, pair
        else:
            src, dst, to = pair_slot, relay_slot, relay_to
        return pltpu.make_async_remote_copy(
            src_ref=win[turn].at[span(src, j)], dst_ref=win[turn].at[span(dst, j)],
            send_sem=band_send.at[stage, kind, turn, j], recv_sem=band_recv.at[stage, kind, turn, j],
            device_id={"blk": to}, device_id_type=MESH,
        )

    def core_copy(win, stage, kind, turn, j):
        if kind == 0:
            src, dst = own_slot, own_dst
        else:
            src, dst = ahead_slot, ahead_dst
        return pltpu.make_async_remote_copy(
            src_ref=win[turn].at[span(src, j)], dst_ref=win[turn].at[span(dst, j)],
            send_sem=core_send.at[stage, kind, turn, j], recv_sem=core_recv.at[stage, kind, turn, j],
            device_id={"blk": other}, device_id_type=MESH,
        )

    def side_copy(ref, k, d):
        return pltpu.make_async_remote_copy(
            src_ref=ref, dst_ref=ref, send_sem=side_send.at[k, d - 1], recv_sem=side_recv.at[k, d - 1],
            device_id={"help": helper_at(d)}, device_id_type=MESH,
        )

    def cot_copy(d):
        return side_copy(cot_all.at[:, mine, :], 0, d)

    def bias_copy(d):
        return side_copy(bias_all.at[mine, :], 1, d)

    def part_copy(h, j, d):
        piece = pl.ds(j * per, per)
        return pltpu.make_async_remote_copy(
            src_ref=part.at[h, piece], dst_ref=part_in.at[d - 1, h, piece],
            send_sem=help_send.at[h, j, d - 1], recv_sem=help_recv.at[h, j, d - 1],
            device_id={"help": helper_at(d)}, device_id_type=MESH,
        )

    def back_copy(j, d):
        theirs = pl.ds(pl.multiple_of(helper_at(d) * share, share), share)
        piece = pl.ds(j * per, per)
        return pltpu.make_async_remote_copy(
            src_ref=part2.at[piece, theirs, :], dst_ref=part2_in.at[d - 1, piece],
            send_sem=back_send.at[j, d - 1], recv_sem=back_recv.at[j, d - 1],
            device_id={"help": helper_at(d)}, device_id_type=MESH,
        )

    def wg_copy(step):
        return pltpu.make_async_remote_copy(
            src_ref=wg.at[step], dst_ref=wg_in.at[step],
            send_sem=wg_send.at[step], recv_sem=wg_recv.at[step],
            device_id={"blk": flip(step)}, device_id_type=MESH,
        )

    def launch(win, stage, k):
        band_copy(win, stage, 0, k // chunks, k % chunks).start()
        core_copy(win, stage, 0, k // chunks, k % chunks).start()

    def pass_on(win, stage, k, more=True):
        turn, j = k // chunks, k % chunks
        band_copy(win, stage, 0, turn, j).wait_recv()
        band_copy(win, stage, 1, turn, j).start()
        band_copy(win, stage, 0, turn, j).wait_send()
        if more and k + AHEAD < HALVES * chunks:
            launch(win, stage, k + AHEAD)

    for copy in small:
        copy.start()
    weight_copy.start()
    for t in range(row_tiles):
        cot_load(t).start()
    tile_copy.start()
    for h in range(HALVES):
        for j in range(chunks):
            feat_copy(h, j).wait()
            for t in range(j * per, (j + 1) * per):
                win1[h][own_slot * row_tiles + t] = feat[h * half : (h + 1) * half, lanes(t)].T
            if h == 0 and j == 0:
                pl.semaphore_wait(barrier, len(peers) + n_help - 1)
            if h * chunks + j < AHEAD:
                launch(win1, 0, h * chunks + j)
    for copy in small:
        copy.wait()
    fill_table(rows, cols, table)
    table_copy.start()
    across = lax.broadcasted_iota(jnp.int32, (share, share), 1)
    along = lax.broadcasted_iota(jnp.int32, (share, share), 0)
    spread = jnp.sum(jnp.where(across == along, bias[...], 0.0), axis=1, keepdims=True)
    bias_all[mine, :] = jnp.broadcast_to(spread, (share, tile))
    for t in range(row_tiles):
        cot_load(t).wait()
    for d in range(1, n_help):
        cot_copy(d).start()
        bias_copy(d).start()
    weight_copy.wait()
    for h, place in ((0, turn_half[0]), (1, own_half)):
        w_t[:, pl.ds(pl.multiple_of(place * half, half), half)] = weight[h * half : (h + 1) * half, :].T
    wg[0] = jnp.zeros_like(wg.at[0])

    def settle(win, stage, turn):
        for j in range(chunks):
            band_copy(win, stage, 1, turn, j).wait_recv()
            core_copy(win, stage, 1, turn, j).start()
        for j in range(chunks):
            core_copy(win, stage, 0, turn, j).wait_recv()
            core_copy(win, stage, 1, turn, j).wait_recv()

    groups = slots // UNROLL
    marks = [i * groups // chunks for i in range(chunks + 1)]

    def aggregate(win, turn, between):
        def body(group, total):
            for u in range(UNROLL):
                t = group * UNROLL + u
                product = jnp.dot(tiles[meta[0, t]], win[turn][meta[1, t]], preferred_element_type=F32)
                total = total * meta[2, t].astype(F32) + product
                seg[turn, t] = total
            return total

        total = jnp.zeros((tile, half), F32)
        for i in range(chunks):
            total = lax.fori_loop(marks[i], marks[i + 1], body, total)
            between(i)

    def row_sum(turn, r):
        return seg[turn, meta[3, r]] * meta[4, r].astype(F32)

    def nothing(i):
        pass

    def send_part(h):
        for j in range(chunks):
            for r in range(j * per, (j + 1) * per):
                part[h, r] = row_sum(h, r).astype(BF16)
            if h == 0 or j < AHEAD:
                for d in range(1, n_help):
                    part_copy(h, j, d).start()

    for j in range(chunks):
        pass_on(win1, 0, j)
    settle(win1, 0, 0)
    tile_copy.wait()
    table_copy.wait()
    aggregate(win1, 0, lambda i: pass_on(win1, 0, chunks + i))
    send_part(0)
    for d in range(1, n_help):
        cot_copy(d).wait_recv()
        bias_copy(d).wait_recv()
    for t in range(row_tiles):
        cot[t] = cot_all[t].T
    bias_wide[...] = bias_all[...].T
    settle(win1, 0, 1)
    aggregate(win1, 1, nothing)
    send_part(1)

    for j in range(chunks):
        for h in range(HALVES):
            for d in range(1, n_help):
                part_copy(h, j, d).wait_recv()
        for d in range(1, n_help):
            part_copy(1, j, d).wait_send()
            if j + AHEAD < chunks:
                part_copy(1, j + AHEAD, d).start()
        for r in range(j * per, (j + 1) * per):
            pieces = []
            for h in range(HALVES):
                total = row_sum(h, r)
                for d in range(1, n_help):
                    total = total + part_in[d - 1, h, r].astype(F32)
                pieces.append(total.astype(BF16))
            agg = jnp.concatenate(pieces, axis=1)
            pre = jnp.dot(agg, weight[...], preferred_element_type=F32) + bias_wide[...]
            ex = jnp.exp(jnp.minimum(pre, 0.0))
            grad = (cot[r].astype(F32) * ex).astype(BF16)
            back = jnp.dot(grad, w_t[...], preferred_element_type=F32).astype(BF16)
            for h in range(HALVES):
                win2[h][own_slot * row_tiles + r] = back[:, h * half : (h + 1) * half]
            out_all[r] = jnp.where(pre > 0.0, pre, ex - 1.0).astype(BF16).T
            gp_all[r] = grad.T
            held = gp_all[r, mine, :]
            wg[0, :, pl.ds(0, width)] += jnp.dot(held, agg, preferred_element_type=F32)
            wg[0, :, pl.ds(width, tile)] += held.astype(F32)
        launch(win2, 1, j)
        if j > 0:
            pass_on(win2, 1, j - 1, False)
    launch(win2, 1, chunks)
    pass_on(win2, 1, chunks - 1)
    wg_copy(0).start()
    for t in range(row_tiles):
        out_ref[:, lanes(t)] = out_all[t, mine, :]

    def wg_turn(step):
        wg_copy(step).wait_recv()
        wg[step + 1] = wg[step] + wg_in[step]
        if step + 1 < steps:
            wg_copy(step + 1).start()

    def keep_sums(turn, early):
        for j in range(chunks):
            for r in range(j * per, (j + 1) * per):
                turned = row_sum(turn, r).T
                place = pl.ds(pl.multiple_of(turn_half[turn] * half, half), half)
                part2[r, place, :] = turned.astype(BF16)
                sums[r, place, :] = turned
            if early:
                for d in range(1, n_help):
                    back_copy(j, d).start()

    settle(win2, 1, 0)
    wg_turn(0)
    aggregate(win2, 0, lambda i: pass_on(win2, 1, chunks + i))
    keep_sums(0, n_help == HALVES)
    wg_turn(1)
    settle(win2, 1, 1)
    aggregate(win2, 1, nothing)
    wg_turn(2)
    keep_sums(1, n_help != HALVES)
    for j in range(chunks):
        for d in range(1, n_help):
            back_copy(j, d).wait_recv()
        for r in range(j * per, (j + 1) * per):
            total = sums[r, mine, :]
            for d in range(1, n_help):
                total = total + part2_in[d - 1, r].astype(F32)
            prop_ref[:, lanes(r)] = total
    for s in range(3, steps):
        wg_turn(s)
    grads_ref[...] = wg[steps]

    for stage, win in ((0, win1), (1, win2)):
        for j in range(chunks):
            for turn in range(HALVES):
                band_copy(win, stage, 1, turn, j).wait_send()
                for kind in range(2):
                    core_copy(win, stage, kind, turn, j).wait_send()
    for d in range(1, n_help):
        cot_copy(d).wait_send()
        bias_copy(d).wait_send()
        for j in range(chunks):
            part_copy(0, j, d).wait_send()
            back_copy(j, d).wait_send()
    for s in range(steps):
        wg_copy(s).wait_send()


def fill_table(rows, cols, table):
    slots = rows.shape[1]
    shape = (slots, slots)
    here = lax.broadcasted_iota(jnp.int32, shape, 0)
    there = lax.broadcasted_iota(jnp.int32, shape, 1)
    zero = jnp.zeros(shape, jnp.int32)
    one = zero + 1

    def upright(line):
        return jnp.sum(jnp.where(here == there, line, zero), axis=1, keepdims=True)

    def flat(mask, values):
        return jnp.sum(jnp.where(mask, values, zero), axis=0, keepdims=True)

    row_l = jnp.broadcast_to(rows[...], shape)
    row_s = jnp.broadcast_to(upright(row_l), shape)
    col_s = jnp.broadcast_to(upright(jnp.broadcast_to(cols[...], shape)), shape)
    before = row_l * slots + there < row_s * slots + here
    rank = jnp.broadcast_to(jnp.sum(jnp.where(before, one, zero), axis=1, keepdims=True), shape)
    placed = rank == there
    table[...] = jnp.zeros(table.shape, jnp.int32)
    table[0:1, 0:slots] = flat(placed, here)
    table[1:2, 0:slots] = flat(placed, col_s)
    goes_on = flat(placed, row_s) == flat(rank + 1 == there, row_s)
    table[2:3, 0:slots] = jnp.where(goes_on, 1, 0)
    table[3:4, 0:slots] = jnp.maximum(flat(row_s <= there, one) - 1, 0)
    table[4:5, 0:slots] = jnp.minimum(flat(row_s == there, one), 1)


def finish_kernel(pieces, scale, out_in, prop_in, grads, out_ref, prop_ref, weight_grad, bias_grad, out_sem, prop_sem):
    rows = out_in.shape[0] // pieces
    width = weight_grad.shape[0]
    copies = []
    for i in range(pieces):
        part = pl.ds(i * rows, rows)
        copies.append(pltpu.make_async_copy(out_in.at[part], out_ref.at[part], out_sem.at[i]))
        copies.append(pltpu.make_async_copy(prop_in.at[part], prop_ref.at[part], prop_sem.at[i]))
    for copy in copies:
        copy.start()
    weight_grad[...] = grads[:, 0:width].T * scale
    bias_grad[...] = jnp.sum(grads[:, width:].T, axis=0, keepdims=True) * scale
    for copy in copies:
        copy.wait()


def per_device(n_blk, n_help, features_t, weight, bias, cotangent_t, tile_vals, slot_row, slot_col):
    tiles = tile_vals[0, 0]
    slots, tile = tiles.shape[0], tiles.shape[-1]
    width, nodes = features_t.shape
    half = width // HALVES
    row_tiles = nodes // tile
    share = cotangent_t.shape[0]
    chunks = 4 if row_tiles % 4 == 0 else 1
    steps = n_blk.bit_length() - 1
    peers = n_help - 1
    vmem = pl.BlockSpec(memory_space=pltpu.VMEM)
    dma = pltpu.SemaphoreType.DMA
    output_t, propagated, grads = pl.pallas_call(
        functools.partial(layer_kernel, n_blk, n_help, chunks),
        out_shape=(
            jax.ShapeDtypeStruct((share, nodes), BF16),
            jax.ShapeDtypeStruct((share, nodes), F32),
            jax.ShapeDtypeStruct((share, width + tile), F32),
        ),
        in_specs=[pl.BlockSpec(memory_space=pltpu.HBM)] * 7,
        out_specs=(vmem, vmem, vmem),
        scratch_shapes=[
            pltpu.VMEM((1, slots), jnp.int32),
            pltpu.VMEM((1, slots), jnp.int32),
            pltpu.VMEM((1, share), F32),
            pltpu.VMEM((8, 128), jnp.int32),
            pltpu.SMEM((8, 128), jnp.int32),
            pltpu.VMEM((width, nodes), BF16),
            pltpu.VMEM((width, width), BF16),
            pltpu.VMEM((tile, width), F32),
            pltpu.VMEM((row_tiles, tile, width), BF16),
            *[pltpu.VMEM((SPANS * row_tiles, tile, half), BF16)] * (2 * HALVES),
            pltpu.VMEM((slots, tile, tile), BF16),
            pltpu.VMEM((HALVES, slots, tile, half), F32),
            pltpu.VMEM((HALVES, row_tiles, tile, half), BF16),
            pltpu.VMEM((peers, HALVES, row_tiles, tile, half), BF16),
            pltpu.VMEM((row_tiles, width, tile), BF16),
            pltpu.VMEM((peers, row_tiles, share, tile), BF16),
            pltpu.VMEM((width, tile), F32),
            pltpu.VMEM((row_tiles, width, tile), BF16),
            pltpu.VMEM((row_tiles, width, tile), BF16),
            pltpu.VMEM((row_tiles, width, tile), BF16),
            pltpu.VMEM((width, width), BF16),
            pltpu.VMEM((steps + 1, share, width + tile), F32),
            pltpu.VMEM((steps, share, width + tile), F32),
            pltpu.VMEM((row_tiles, width, tile), F32),
            dma((4,)),
            dma((HALVES, chunks)),
            dma,
            dma,
            dma((row_tiles,)),
            dma((2, 2, HALVES, chunks)),
            dma((2, 2, HALVES, chunks)),
            dma((2, 2, HALVES, chunks)),
            dma((2, 2, HALVES, chunks)),
            dma((HALVES, chunks, peers)),
            dma((HALVES, chunks, peers)),
            dma((2, peers)),
            dma((2, peers)),
            dma((chunks, peers)),
            dma((chunks, peers)),
            dma((steps,)),
            dma((steps,)),
        ],
        compiler_params=pltpu.CompilerParams(
            collective_id=0, has_side_effects=True, vmem_limit_bytes=VMEM_MIB * 1024 * 1024
        ),
    )(slot_row[0], slot_col[0], features_t, weight, bias.reshape(1, share), cotangent_t, tiles)
    scale = 1.0 / math.sqrt(nodes * n_blk)
    anywhere = pl.BlockSpec(memory_space=pltpu.HBM)
    pieces = 4 if share % 64 == 0 else 2
    output_t, propagated, weight_grad, bias_grad = pl.pallas_call(
        functools.partial(finish_kernel, pieces, scale),
        out_shape=(
            jax.ShapeDtypeStruct((share, nodes), BF16),
            jax.ShapeDtypeStruct((share, nodes), F32),
            jax.ShapeDtypeStruct((width, share), F32),
            jax.ShapeDtypeStruct((1, share), F32),
        ),
        in_specs=[anywhere, anywhere, vmem],
        out_specs=(anywhere, anywhere, vmem, vmem),
        scratch_shapes=[dma((pieces,)), dma((pieces,))],
        compiler_params=pltpu.CompilerParams(vmem_limit_bytes=VMEM_MIB * 1024 * 1024),
    )(output_t, propagated, grads)
    return (output_t, propagated, weight_grad, bias_grad.reshape(share))


def solution(mesh):
    placed = (
        P(None, "blk"),
        P(),
        P("help"),
        P("help", "blk"),
        P("blk", "help", None, None, None),
        P("blk", "help", None),
        P("blk", "help", None),
    )
    return jax.shard_map(
        functools.partial(per_device, mesh.shape["blk"], mesh.shape["help"]),
        mesh=mesh,
        in_specs=placed,
        out_specs=(P("help", "blk"), P("help", "blk"), P(None, "help"), P("help")),
        check_vma=False,
    )
```

```python
import functools
import math

import jax
import jax.numpy as jnp
from jax import lax
from jax.experimental import pallas as pl
from jax.experimental.pallas import tpu as pltpu
from jax.sharding import PartitionSpec as P

BAND = 2
SPANS = 2 * BAND + 1
UNROLL = 4
QUAD = 4
HALVES = 2
VMEM_MIB = 60
MESH = pl.DeviceIdType.MESH
F32 = jnp.float32
BF16 = jnp.bfloat16


def layer_kernel(
    n_blk, n_help, chunks,
    rows_hbm, cols_hbm, feat_hbm, weight_hbm, bias_hbm, cot_hbm, tiles_hbm,
    out_ref, prop_ref, grads_ref,
    rows, cols, bias, table, meta, feat, weight, bias_wide, cot,
    win1a, win1b, win2a, win2b, tiles, seg, part, part_in, part2, part2_in, bias_all, cot_all, gp_all, out_all, w_t, wg, wg_in,
    sums, small_sem, feat_sem, tile_sem, weight_sem, cot_sem,
    band_send, band_recv, core_send, core_recv, help_send, help_recv, side_send, side_recv,
    back_send, back_recv, wg_send, wg_recv,
):
    blk = lax.axis_index("blk")
    helper = lax.axis_index("help")
    row_tiles = feat.shape[1] // tiles.shape[-1]
    slots = tiles_hbm.shape[0]
    tile = tiles.shape[-1]
    width = weight.shape[0]
    half = width // HALVES
    share = out_ref.shape[0]
    per = row_tiles // chunks
    steps = n_blk.bit_length() - 1
    core = lax.rem(blk, 2)
    chip = blk // 2
    odd = lax.rem(chip, 2)
    pair = blk + 2 - 4 * odd
    up = lax.rem(blk + 4, n_blk)
    down = lax.rem(blk + n_blk - 4, n_blk)
    relay_to = up + odd * (down - up)
    other = blk + 1 - 2 * core
    own_slot = BAND
    pair_slot = 4 - 4 * odd
    relay_slot = 4 * odd
    ahead_slot = 4 - 4 * core
    own_dst = 1 + 2 * core
    ahead_dst = 3 - 2 * core
    own_half = (helper * share) // half
    turn_half = (1 - own_half, own_half)
    win1, win2 = (win1a, win1b), (win2a, win2b)

    def flip(step):
        bit = 1 << step
        return blk + bit - 2 * bit * lax.rem(blk // bit, 2)

    def helper_at(distance):
        return lax.rem(helper + distance, n_help)

    def lanes(t):
        return slice(t * tile, (t + 1) * tile)

    mine = pl.ds(pl.multiple_of(helper * share, share), share)

    def feat_copy(h, j):
        piece = (slice(h * half, (h + 1) * half), slice(j * per * tile, (j + 1) * per * tile))
        return pltpu.make_async_copy(feat_hbm.at[piece], feat.at[piece], feat_sem.at[h, j])

    def cot_load(t):
        return pltpu.make_async_copy(cot_hbm.at[:, lanes(t)], cot_all.at[t, mine, :], cot_sem.at[t])

    for h in range(HALVES):
        for j in range(chunks):
            feat_copy(h, j).start()
    peers = [up, down, pair] + [flip(s) for s in range(steps) if s != 1]
    barrier = pltpu.get_barrier_semaphore()
    for peer in peers:
        pl.semaphore_signal(barrier, inc=1, device_id={"blk": peer}, device_id_type=MESH)
    for d in range(1, n_help):
        pl.semaphore_signal(barrier, inc=1, device_id={"help": helper_at(d)}, device_id_type=MESH)
    small = [
        pltpu.make_async_copy(rows_hbm, rows, small_sem.at[0]),
        pltpu.make_async_copy(cols_hbm, cols, small_sem.at[1]),
        pltpu.make_async_copy(bias_hbm, bias, small_sem.at[2]),
    ]
    table_copy = pltpu.make_async_copy(table, meta, small_sem.at[3])
    tile_copy = pltpu.make_async_copy(tiles_hbm, tiles.at[pl.ds(0, slots)], tile_sem)
    weight_copy = pltpu.make_async_copy(weight_hbm, weight, weight_sem)

    def span(slot, j):
        return pl.ds(slot * row_tiles + j * per, per)

    def band_copy(win, stage, kind, turn, j):
        if kind == 0:
            src, dst, to = own_slot, relay_slot, pair
        else:
            src, dst, to = pair_slot, relay_slot, relay_to
        return pltpu.make_async_remote_copy(
            src_ref=win[turn].at[span(src, j)], dst_ref=win[turn].at[span(dst, j)],
            send_sem=band_send.at[stage, kind, turn, j], recv_sem=band_recv.at[stage, kind, turn, j],
            device_id={"blk": to}, device_id_type=MESH,
        )

    def core_copy(win, stage, kind, turn, j):
        if kind == 0:
            src, dst = own_slot, own_dst
        else:
            src, dst = ahead_slot, ahead_dst
        return pltpu.make_async_remote_copy(
            src_ref=win[turn].at[span(src, j)], dst_ref=win[turn].at[span(dst, j)],
            send_sem=core_send.at[stage, kind, turn, j], recv_sem=core_recv.at[stage, kind, turn, j],
            device_id={"blk": other}, device_id_type=MESH,
        )

    def side_copy(ref, k, d):
        return pltpu.make_async_remote_copy(
            src_ref=ref, dst_ref=ref, send_sem=side_send.at[k, d - 1], recv_sem=side_recv.at[k, d - 1],
            device_id={"help": helper_at(d)}, device_id_type=MESH,
        )

    def cot_copy(d):
        return side_copy(cot_all.at[:, mine, :], 0, d)

    def bias_copy(d):
        return side_copy(bias_all.at[mine, :], 1, d)

    def part_copy(h, j, d):
        piece = pl.ds(j * per, per)
        return pltpu.make_async_remote_copy(
            src_ref=part.at[h, piece], dst_ref=part_in.at[d - 1, h, piece],
            send_sem=help_send.at[h, j, d - 1], recv_sem=help_recv.at[h, j, d - 1],
            device_id={"help": helper_at(d)}, device_id_type=MESH,
        )

    def back_copy(j, d):
        theirs = pl.ds(pl.multiple_of(helper_at(d) * share, share), share)
        piece = pl.ds(j * per, per)
        return pltpu.make_async_remote_copy(
            src_ref=part2.at[piece, theirs, :], dst_ref=part2_in.at[d - 1, piece],
            send_sem=back_send.at[j, d - 1], recv_sem=back_recv.at[j, d - 1],
            device_id={"help": helper_at(d)}, device_id_type=MESH,
        )

    def wg_copy(step):
        return pltpu.make_async_remote_copy(
            src_ref=wg.at[step], dst_ref=wg_in.at[step],
            send_sem=wg_send.at[step], recv_sem=wg_recv.at[step],
            device_id={"blk": flip(step)}, device_id_type=MESH,
        )

    for copy in small:
        copy.start()
    weight_copy.start()
    for t in range(row_tiles):
        cot_load(t).start()
    tile_copy.start()
    for h in range(HALVES):
        for j in range(chunks):
            feat_copy(h, j).wait()
            for t in range(j * per, (j + 1) * per):
                win1[h][own_slot * row_tiles + t] = feat[h * half : (h + 1) * half, lanes(t)].T
            if h == 0 and j == 0:
                pl.semaphore_wait(barrier, len(peers) + n_help - 1)
            band_copy(win1, 0, 0, h, j).start()
        for j in range(chunks):
            core_copy(win1, 0, 0, h, j).start()
    for copy in small:
        copy.wait()
    tiles[slots] = jnp.zeros((tile, tile), BF16)
    fill_table(rows, cols, table, row_tiles)
    table_copy.start()
    across = lax.broadcasted_iota(jnp.int32, (share, share), 1)
    along = lax.broadcasted_iota(jnp.int32, (share, share), 0)
    spread = jnp.sum(jnp.where(across == along, bias[...], 0.0), axis=1, keepdims=True)
    bias_all[mine, :] = jnp.broadcast_to(spread, (share, tile))
    for t in range(row_tiles):
        cot_load(t).wait()
    for d in range(1, n_help):
        cot_copy(d).start()
        bias_copy(d).start()
    weight_copy.wait()
    for h, place in ((0, turn_half[0]), (1, own_half)):
        w_t[:, pl.ds(pl.multiple_of(place * half, half), half)] = weight[h * half : (h + 1) * half, :].T
    wg[0] = jnp.zeros_like(wg.at[0])

    def pass_on(win, stage, turn, j):
        band_copy(win, stage, 0, turn, j).wait_recv()
        band_copy(win, stage, 1, turn, j).start()

    def settle(win, stage, turn):
        for j in range(chunks):
            band_copy(win, stage, 1, turn, j).wait_recv()
            core_copy(win, stage, 1, turn, j).start()
        for j in range(chunks):
            core_copy(win, stage, 0, turn, j).wait_recv()
            core_copy(win, stage, 1, turn, j).wait_recv()

    groups = seg.shape[1] // UNROLL
    marks = [i * groups // chunks for i in range(chunks + 1)]

    def aggregate(win, turn, between):
        def body(group, total):
            for u in range(UNROLL):
                t = group * UNROLL + u
                left = jnp.concatenate([tiles[meta[0, t * QUAD + i]] for i in range(QUAD)], axis=1)
                right = jnp.concatenate([win[turn][meta[1, t * QUAD + i]] for i in range(QUAD)], axis=0)
                product = jnp.dot(left, right, preferred_element_type=F32)
                total = total * meta[2, t * QUAD].astype(F32) + product
                seg[turn, t] = total
            return total

        total = jnp.zeros((tile, half), F32)
        for i in range(chunks):
            total = lax.fori_loop(marks[i], marks[i + 1], body, total)
            between(i)

    def row_sum(turn, r):
        return seg[turn, meta[3, r]] * meta[4, r].astype(F32)

    def nothing(i):
        pass

    def send_part(h):
        for j in range(chunks):
            for r in range(j * per, (j + 1) * per):
                part[h, r] = row_sum(h, r).astype(BF16)
            for d in range(1, n_help):
                part_copy(h, j, d).start()

    for j in range(chunks):
        pass_on(win1, 0, 0, j)
    settle(win1, 0, 0)
    tile_copy.wait()
    table_copy.wait()
    aggregate(win1, 0, lambda i: pass_on(win1, 0, 1, i))
    send_part(0)
    for d in range(1, n_help):
        cot_copy(d).wait_recv()
        bias_copy(d).wait_recv()
    for t in range(row_tiles):
        cot[t] = cot_all[t].T
    bias_wide[...] = bias_all[...].T
    settle(win1, 0, 1)
    aggregate(win1, 1, nothing)
    send_part(1)

    for j in range(chunks):
        for h in range(HALVES):
            for d in range(1, n_help):
                part_copy(h, j, d).wait_recv()
        for r in range(j * per, (j + 1) * per):
            pieces = []
            for h in range(HALVES):
                total = row_sum(h, r)
                for d in range(1, n_help):
                    total = total + part_in[d - 1, h, r].astype(F32)
                pieces.append(total.astype(BF16))
            agg = jnp.concatenate(pieces, axis=1)
            pre = jnp.dot(agg, weight[...], preferred_element_type=F32) + bias_wide[...]
            ex = jnp.exp(jnp.minimum(pre, 0.0))
            grad = (cot[r].astype(F32) * ex).astype(BF16)
            back = jnp.dot(grad, w_t[...], preferred_element_type=F32).astype(BF16)
            for h in range(HALVES):
                win2[h][own_slot * row_tiles + r] = back[:, h * half : (h + 1) * half]
            out_all[r] = jnp.where(pre > 0.0, pre, ex - 1.0).astype(BF16).T
            gp_all[r] = grad.T
            held = gp_all[r, mine, :]
            wg[0, :, pl.ds(0, width)] += jnp.dot(held, agg, preferred_element_type=F32)
            wg[0, :, pl.ds(width, tile)] += held.astype(F32)
        band_copy(win2, 1, 0, 0, j).start()
        core_copy(win2, 1, 0, 0, j).start()
        if j > 0:
            pass_on(win2, 1, 0, j - 1)
    for j in range(chunks):
        band_copy(win2, 1, 0, 1, j).start()
        core_copy(win2, 1, 0, 1, j).start()
    pass_on(win2, 1, 0, chunks - 1)
    wg_copy(0).start()
    for t in range(row_tiles):
        out_ref[:, lanes(t)] = out_all[t, mine, :]

    def wg_turn(step):
        wg_copy(step).wait_recv()
        wg[step + 1] = wg[step] + wg_in[step]
        if step + 1 < steps:
            wg_copy(step + 1).start()

    def keep_sums(turn, early):
        for j in range(chunks):
            for r in range(j * per, (j + 1) * per):
                turned = row_sum(turn, r).T
                place = pl.ds(pl.multiple_of(turn_half[turn] * half, half), half)
                part2[r, place, :] = turned.astype(BF16)
                sums[r, place, :] = turned
            if early:
                for d in range(1, n_help):
                    back_copy(j, d).start()

    settle(win2, 1, 0)
    wg_turn(0)
    aggregate(win2, 0, lambda i: pass_on(win2, 1, 1, i))
    keep_sums(0, n_help == HALVES)
    wg_turn(1)
    settle(win2, 1, 1)
    aggregate(win2, 1, nothing)
    wg_turn(2)
    keep_sums(1, n_help != HALVES)
    for j in range(chunks):
        for d in range(1, n_help):
            back_copy(j, d).wait_recv()
        for r in range(j * per, (j + 1) * per):
            total = sums[r, mine, :]
            for d in range(1, n_help):
                total = total + part2_in[d - 1, r].astype(F32)
            prop_ref[:, lanes(r)] = total
    for s in range(3, steps):
        wg_turn(s)
    grads_ref[...] = wg[steps]

    for stage, win in ((0, win1), (1, win2)):
        for j in range(chunks):
            for kind in range(2):
                for turn in range(HALVES):
                    band_copy(win, stage, kind, turn, j).wait_send()
                    core_copy(win, stage, kind, turn, j).wait_send()
    for d in range(1, n_help):
        cot_copy(d).wait_send()
        bias_copy(d).wait_send()
        for j in range(chunks):
            for h in range(HALVES):
                part_copy(h, j, d).wait_send()
            back_copy(j, d).wait_send()
    for s in range(steps):
        wg_copy(s).wait_send()


def fill_table(rows, cols, table, row_tiles):
    slots = rows.shape[1]
    places = table.shape[1]
    shape = (slots, slots)
    wide = (slots, places)
    here = lax.broadcasted_iota(jnp.int32, shape, 0)
    there = lax.broadcasted_iota(jnp.int32, shape, 1)
    zero = jnp.zeros(shape, jnp.int32)
    one = zero + 1
    place = lax.broadcasted_iota(jnp.int32, wide, 1)
    slot = lax.broadcasted_iota(jnp.int32, wide, 0)
    none = jnp.zeros(wide, jnp.int32)

    def upright(mask, values):
        return jnp.sum(jnp.where(mask, values, zero), axis=1, keepdims=True)

    def flat(mask, values):
        return jnp.sum(jnp.where(mask, values, zero), axis=0, keepdims=True)

    def flat_wide(mask, values):
        return jnp.sum(jnp.where(mask, values, none), axis=0, keepdims=True)

    row_l = jnp.broadcast_to(rows[...], shape)
    row_u = upright(here == there, row_l)
    row_s = jnp.broadcast_to(row_u, shape)
    row_w = jnp.broadcast_to(row_u, wide)
    col_w = jnp.broadcast_to(upright(here == there, jnp.broadcast_to(cols[...], shape)), wide)
    count = flat(row_s == there, one)
    filled = jnp.broadcast_to(jnp.bitwise_and(count + (QUAD - 1), -QUAD), shape)
    head = upright((row_l == row_s) & (there < here), one)
    start = upright(there < row_s, filled)
    spot = jnp.where(row_w < row_tiles, jnp.broadcast_to(start + head, wide), none - 2 * QUAD)
    filled_s = jnp.broadcast_to(upright(here == there, filled), shape)
    placed = spot == place
    table[...] = jnp.zeros(table.shape, jnp.int32)
    table[0:1, :] = flat_wide(placed, slot - slots) + slots
    table[1:2, :] = flat_wide(placed, col_w)
    goes_on = flat_wide(placed, row_w) == flat_wide(spot + QUAD == place, row_w)
    table[2:3, :] = jnp.where(goes_on, 1, 0)
    table[3:4, 0:slots] = jnp.maximum(jnp.right_shift(flat(here <= there, filled_s), 2) - 1, 0)
    table[4:5, 0:slots] = jnp.minimum(count, 1)


def finish_kernel(scale, out_in, prop_in, grads, out_ref, prop_ref, weight_grad, bias_grad):
    width = weight_grad.shape[0]
    out_ref[...] = out_in[...]
    prop_ref[...] = prop_in[...]
    weight_grad[...] = grads[:, 0:width].T * scale
    bias_grad[...] = jnp.sum(grads[:, width:].T, axis=0, keepdims=True) * scale


def per_device(n_blk, n_help, features_t, weight, bias, cotangent_t, tile_vals, slot_row, slot_col):
    tiles = tile_vals[0, 0]
    slots, tile = tiles.shape[0], tiles.shape[-1]
    width, nodes = features_t.shape
    half = width // HALVES
    row_tiles = nodes // tile
    share = cotangent_t.shape[0]
    chunks = 4 if row_tiles % 4 == 0 else 1
    quads = -(-(slots + row_tiles * (QUAD - 1)) // (QUAD * UNROLL * chunks)) * UNROLL * chunks
    steps = n_blk.bit_length() - 1
    peers = n_help - 1
    vmem = pl.BlockSpec(memory_space=pltpu.VMEM)
    dma = pltpu.SemaphoreType.DMA
    output_t, propagated, grads = pl.pallas_call(
        functools.partial(layer_kernel, n_blk, n_help, chunks),
        out_shape=(
            jax.ShapeDtypeStruct((share, nodes), BF16),
            jax.ShapeDtypeStruct((share, nodes), F32),
            jax.ShapeDtypeStruct((share, width + tile), F32),
        ),
        in_specs=[pl.BlockSpec(memory_space=pltpu.HBM)] * 7,
        out_specs=(vmem, vmem, vmem),
        scratch_shapes=[
            pltpu.VMEM((1, slots), jnp.int32),
            pltpu.VMEM((1, slots), jnp.int32),
            pltpu.VMEM((1, share), F32),
            pltpu.VMEM((8, 128), jnp.int32),
            pltpu.SMEM((8, 128), jnp.int32),
            pltpu.VMEM((width, nodes), BF16),
            pltpu.VMEM((width, width), BF16),
            pltpu.VMEM((tile, width), F32),
            pltpu.VMEM((row_tiles, tile, width), BF16),
            *[pltpu.VMEM((SPANS * row_tiles, tile, half), BF16)] * (2 * HALVES),
            pltpu.VMEM((slots + 1, tile, tile), BF16),
            pltpu.VMEM((HALVES, quads, tile, half), F32),
            pltpu.VMEM((HALVES, row_tiles, tile, half), BF16),
            pltpu.VMEM((peers, HALVES, row_tiles, tile, half), BF16),
            pltpu.VMEM((row_tiles, width, tile), BF16),
            pltpu.VMEM((peers, row_tiles, share, tile), BF16),
            pltpu.VMEM((width, tile), F32),
            pltpu.VMEM((row_tiles, width, tile), BF16),
            pltpu.VMEM((row_tiles, width, tile), BF16),
            pltpu.VMEM((row_tiles, width, tile), BF16),
            pltpu.VMEM((width, width), BF16),
            pltpu.VMEM((steps + 1, share, width + tile), F32),
            pltpu.VMEM((steps, share, width + tile), F32),
            pltpu.VMEM((row_tiles, width, tile), F32),
            dma((4,)),
            dma((HALVES, chunks)),
            dma,
            dma,
            dma((row_tiles,)),
            dma((2, 2, HALVES, chunks)),
            dma((2, 2, HALVES, chunks)),
            dma((2, 2, HALVES, chunks)),
            dma((2, 2, HALVES, chunks)),
            dma((HALVES, chunks, peers)),
            dma((HALVES, chunks, peers)),
            dma((2, peers)),
            dma((2, peers)),
            dma((chunks, peers)),
            dma((chunks, peers)),
            dma((steps,)),
            dma((steps,)),
        ],
        compiler_params=pltpu.CompilerParams(
            collective_id=0, has_side_effects=True, vmem_limit_bytes=VMEM_MIB * 1024 * 1024
        ),
    )(slot_row[0], slot_col[0], features_t, weight, bias.reshape(1, share), cotangent_t, tiles)
    scale = 1.0 / math.sqrt(nodes * n_blk)
    output_t, propagated, weight_grad, bias_grad = pl.pallas_call(
        functools.partial(finish_kernel, scale),
        out_shape=(
            jax.ShapeDtypeStruct((share, nodes), BF16),
            jax.ShapeDtypeStruct((share, nodes), F32),
            jax.ShapeDtypeStruct((width, share), F32),
            jax.ShapeDtypeStruct((1, share), F32),
        ),
        in_specs=[vmem] * 3,
        out_specs=(vmem,) * 4,
        compiler_params=pltpu.CompilerParams(vmem_limit_bytes=VMEM_MIB * 1024 * 1024),
    )(output_t, propagated, grads)
    return (output_t, propagated, weight_grad, bias_grad.reshape(share))


def solution(mesh):
    placed = (
        P(None, "blk"),
        P(),
        P("help"),
        P("help", "blk"),
        P("blk", "help", None, None, None),
        P("blk", "help", None),
        P("blk", "help", None),
    )
    return jax.shard_map(
        functools.partial(per_device, mesh.shape["blk"], mesh.shape["help"]),
        mesh=mesh,
        in_specs=placed,
        out_specs=(P("help", "blk"), P("help", "blk"), P(None, "help"), P("help")),
        check_vma=False,
    )
```
